128 devices in a mesh: section: 8 (over z, core), group: 16 (over x, y).
Axes of the slice: x: 4, y: 4, z: 4, core: 2. Of those that a mesh axis runs over, the one named last changes fastest.
Arguments:
- features: bfloat16 [65536, 256], P('group'), may hold values from -6 to 6
- history: bfloat16 [8, 65536, 256], P('section', 'group'), may hold values from -6 to 6
- halo_blocks: int32 [16, 16, 1], P('group'), may hold values from 0 to 31
- tile_values: bfloat16 [128, 32, 128, 128], P('group'), may hold values from -0.1875 to 0.1875
- tile_dst: int32 [128, 32], P('group'), may hold values from 0 to 3
- tile_src: int32 [128, 32], P('group'), may hold values from 0 to 19
- w_self: bfloat16 [8, 256, 256], P('section'), may hold values from -0.375 to 0.375
- w_neigh: bfloat16 [8, 256, 256], P('section'), may hold values from -0.375 to 0.375
- bias: float32 [8, 256], P('section'), may hold values from -3 to 3
- gain: float32 [8, 256], P('section'), may hold values from 0.25 to 1.75
Outputs:
- embeddings: bfloat16 [65536, 256], P('group', 'section')
- fresh_history: bfloat16 [8, 65536, 256], P('section', 'group')
The draws below stay inside these ranges and needn't reach their ends.
All inputs are finite; a program needn't handle non-finite values.
Results may differ from the reference program's by a relative error of at most 0.014.
Values may be sent and summed in bfloat16 or wider, within the bound.
A program may use at most 128 MiB of HBM per device.

```python
import jax
import jax.numpy as jnp
from jax import lax

H = 256
TILE = 128
CB = 4
MB = 8
HALO_K = 1
NT = 32
LAYERS = 8
NODES_DEV = 4096
NODES = 65536
N_GROUP = 16


def with_ends(entries, rng, smallest, largest):
    longest = entries.shape.index(max(entries.shape))
    spots = []
    for shift in (0, 1):
        where = [jax.random.randint(jax.random.fold_in(rng, axis), (), 0, length) for axis, length in enumerate(entries.shape)]
        where[longest] = (where[longest] + shift) % entries.shape[longest]
        spots.append(tuple(where))
    return entries.at[spots[0]].set(smallest).at[spots[1]].set(largest)


def shard_levels(stream_key, extent, cuts, low, high):
    def one(position, blocks):
        heights = jax.random.uniform(jax.random.fold_in(jax.random.fold_in(stream_key, 6), position), (blocks,), jnp.float32, low / len(cuts), high / len(cuts))
        return jnp.repeat(jnp.exp(heights), extent[position] // blocks).reshape((-1,) + (1,) * (len(extent) - position - 1))

    factor_of = one(*cuts[0])
    for cut in cuts[1:]:
        factor_of = factor_of * one(*cut)
    return factor_of


def normal_values(own_key, extent, scale, bound, pieces=(), kind=jnp.bfloat16):
    level = shard_levels(own_key, extent, pieces, -0.22, 0.18) if pieces else 1.0
    array = jax.random.normal(own_key, extent, jnp.float32) * scale * level
    return jnp.minimum(jnp.maximum(array, -bound), bound).astype(kind)


def setup_inputs(seed: int = 0) -> dict:
    seeds = jax.random.split(jax.random.key(seed), 11)
    features = normal_values(seeds[0], (NODES, H), 1.0, 6.0, ((0, 16),))
    history = normal_values(seeds[1], (LAYERS, NODES, H), 1.0, 6.0, ((0, 8), (1, 16)))
    halo_blocks = with_ends(jax.random.randint(seeds[2], (N_GROUP, N_GROUP, HALO_K), 0, MB * CB), jax.random.fold_in(seeds[2], 1), 0, (MB * CB) - 1).astype(jnp.int32)
    tile_values = normal_values(seeds[3], (N_GROUP * MB, NT, TILE, TILE), (TILE * NT // CB) ** -0.5, 0.1875, ((0, 16),))
    tile_dst = with_ends(jax.random.randint(seeds[4], (N_GROUP * MB, NT), 0, CB), jax.random.fold_in(seeds[4], 1), 0, CB - 1).astype(jnp.int32)
    tile_src = with_ends(jax.random.randint(seeds[5], (N_GROUP * MB, NT), 0, CB + N_GROUP * HALO_K), jax.random.fold_in(seeds[5], 1), 0, (CB + N_GROUP * HALO_K) - 1).astype(jnp.int32)
    w_self = normal_values(seeds[6], (LAYERS, H, H), H ** -0.5, 0.375, ((0, 8),))
    w_neigh = normal_values(seeds[7], (LAYERS, H, H), H ** -0.5, 0.375, ((0, 8),))
    bias = normal_values(seeds[8], (LAYERS, H), 0.5, 3.0, ((0, 8),), jnp.float32)
    gain = jnp.clip(1.0 + 0.15 * jax.random.normal(seeds[9], (LAYERS, H), jnp.float32), 0.25, 1.75)
    return {"features": features, "history": history, "halo_blocks": halo_blocks, "tile_values": tile_values, "tile_dst": tile_dst, "tile_src": tile_src, "w_self": w_self, "w_neigh": w_neigh, "bias": bias, "gain": gain}


def sage_layer(inputs, halo, tiles, targets, source_ids, weight_self, weight_neigh, bias_row, gain_row):
    width = inputs.shape[1]
    stacked = jnp.concatenate([inputs, halo], axis=0)
    blocks = stacked.reshape(-1, TILE, width)
    picked = jnp.take(blocks, source_ids, axis=0)
    products = jnp.einsum('tij,tjh->tih', tiles.astype(jnp.float32), picked.astype(jnp.float32))
    onehot = (targets[None, :] == jnp.arange(CB, dtype=jnp.int32)[:, None]).astype(jnp.float32)
    aggregate = jnp.einsum('bt,tih->bih', onehot, products).reshape(CB * TILE, width).astype(jnp.bfloat16)
    pre = jnp.dot(inputs, weight_self, preferred_element_type=jnp.float32)
    pre = pre + jnp.dot(aggregate, weight_neigh, preferred_element_type=jnp.float32) + bias_row
    center = pre - lax.optimization_barrier(jnp.mean(pre, axis=1, keepdims=True))
    variance = lax.optimization_barrier(jnp.mean(center * center, axis=1, keepdims=True))
    normed = center * lax.rsqrt(variance + 1e-05) * gain_row
    return (inputs.astype(jnp.float32) + jax.nn.relu(normed)).astype(jnp.bfloat16)

def reference(features, history, halo_blocks, tile_values, tile_dst, tile_src, w_self, w_neigh, bias, gain):
    current = features
    fresh_list = []
    for layer in range(LAYERS):
        fresh_list.append(current)
        table = history[layer]

        def one_group(index):
            wanted = halo_blocks[index]
            starts = jnp.arange(N_GROUP, dtype=jnp.int32)[:, None] * NODES_DEV + wanted * TILE
            row_ids = (starts[:, :, None] + jnp.arange(TILE, dtype=jnp.int32)).reshape(-1)
            halo = jnp.take(table, row_ids, axis=0)
            rows = lax.dynamic_slice_in_dim(current, (index * NODES_DEV).astype(jnp.int32), NODES_DEV, 0)
            rows = rows.reshape(MB, CB * TILE, H)
            results = []
            for micro in range(MB):
                tile_row = (index * MB + micro).astype(jnp.int32)
                tiles = lax.dynamic_index_in_dim(tile_values, tile_row, 0, keepdims=False)
                targets = lax.dynamic_index_in_dim(tile_dst, tile_row, 0, keepdims=False)
                source_ids = lax.dynamic_index_in_dim(tile_src, tile_row, 0, keepdims=False)
                results.append(sage_layer(rows[micro], halo, tiles, targets, source_ids, w_self[layer], w_neigh[layer], bias[layer], gain[layer]))
            return jnp.concatenate(results, axis=0)
        current = lax.map(one_group, jnp.arange(N_GROUP, dtype=jnp.int32)).reshape(NODES, H)
    return (current, jnp.stack(fresh_list))
```

```python
import functools

import jax
import jax.numpy as jnp
from jax import lax
from jax.experimental import pallas as pl
from jax.experimental.pallas import tpu as pltpu
from jax.sharding import PartitionSpec as P

MESH = pl.DeviceIdType.MESH
F32 = jnp.float32
BF16 = jnp.bfloat16
SIDE = 4


def tile_table(targets, sources, blocks, span):
    count = targets.shape[1]
    key = targets * span + sources
    at = jnp.arange(count, dtype=jnp.int32)
    before = (key[:, None, :] < key[:, :, None]) | (
        (key[:, None, :] == key[:, :, None]) & (at[None, None, :] < at[None, :, None])
    )
    rank = jnp.sum(before.astype(jnp.int32), axis=2)
    placed = (rank[:, :, None] == at[None, None, :]).astype(jnp.int32)
    order = jnp.sum(placed * at[None, :, None], axis=1)
    halo = jnp.sum(placed * jnp.maximum(sources - blocks, 0)[:, :, None], axis=1)
    limits = (
        jnp.arange(blocks, dtype=jnp.int32)[:, None] * span
        + jnp.arange(blocks + 1, dtype=jnp.int32)[None, :]
    ).reshape(-1)
    limits = jnp.concatenate([limits, jnp.full((1,), blocks * span, jnp.int32)])
    starts = jnp.sum((key[:, :, None] < limits[None, None, :]).astype(jnp.int32), axis=1)
    return jnp.concatenate([order, halo, starts], axis=1)


def kernel(
    table,
    wanted,
    features,
    history,
    tiles,
    weight_self,
    weight_neigh,
    bias,
    gain,
    emb,
    fresh,
    idx,
    hist_v,
    tiles_v,
    halo_v,
    pack_v,
    dense_v,
    run_tile,
    run_prod,
    agg_v,
    cur_v,
    out_v,
    turn_v,
    ws_v,
    wn_v,
    local_sem,
    fresh_sem,
    own_sem,
    idx_send,
    idx_recv,
    halo_send,
    halo_recv,
    hop_send,
    hop_recv,
    emb_send,
    emb_recv,
):
    section = lax.axis_index("section")
    group = lax.axis_index("group")
    sections = lax.axis_size("section")
    groups = lax.axis_size("group")
    last = sections - 1
    micros = dense_v.shape[0]
    count = tiles_v.shape[0] // micros
    rows = dense_v.shape[1]
    half = rows // 2
    tile = tiles_v.shape[1]
    blocks = rows // tile
    share = emb.shape[0]
    gx, gy = group // SIDE, group % SIDE
    shifts = [(dx, dy) for dx in range(SIDE) for dy in range(SIDE) if dx or dy]

    def peer(shift):
        return ((gx + shift[0]) % SIDE) * SIDE + (gy + shift[1]) % SIDE

    def slot(shift):
        return shift[0] * SIDE + shift[1]

    def back(shift):
        return ((-shift[0]) % SIDE, (-shift[1]) % SIDE)

    hist_in = pltpu.make_async_copy(history, hist_v, local_sem.at[0])
    tiles_in = pltpu.make_async_copy(tiles, tiles_v, local_sem.at[1])
    ws_in = pltpu.make_async_copy(weight_self, ws_v, local_sem.at[2])
    wn_in = pltpu.make_async_copy(weight_neigh, wn_v, local_sem.at[3])
    feat_in = pltpu.make_async_copy(features, cur_v, local_sem.at[4])
    hist_in.start()
    ws_in.start()
    wn_in.start()

    @pl.when(section == 0)
    def _():
        feat_in.start()

    tiles_in.start()

    barrier = pltpu.get_barrier_semaphore()
    for shift in shifts:
        pl.semaphore_signal(barrier, inc=1, device_id={"group": peer(shift)}, device_id_type=MESH)

    @pl.when(section > 0)
    def _():
        pl.semaphore_signal(barrier, inc=1, device_id={"section": section - 1}, device_id_type=MESH)

    @pl.when(section < last)
    def _():
        pl.semaphore_signal(barrier, inc=1, device_id={"section": last}, device_id_type=MESH)
        pl.semaphore_wait(barrier, groups)

    @pl.when(section == last)
    def _():
        pl.semaphore_wait(barrier, groups - 1 + sections - 1)

    def idx_copy(shift, side):
        return pltpu.make_async_remote_copy(
            src_ref=wanted,
            dst_ref=idx.at[group if side == "send" else peer(shift)],
            send_sem=idx_send.at[slot(shift)],
            recv_sem=idx_recv.at[slot(shift if side == "send" else back(shift))],
            device_id={"group": peer(shift)},
            device_id_type=MESH,
        )

    def halo_copy(shift, side):
        return pltpu.make_async_remote_copy(
            src_ref=pack_v.at[slot(shift)],
            dst_ref=halo_v.at[group if side == "send" else peer(shift)],
            send_sem=halo_send.at[slot(shift)],
            recv_sem=halo_recv.at[slot(shift if side == "send" else back(shift))],
            device_id={"group": peer(shift)},
            device_id_type=MESH,
        )

    for shift in shifts:
        idx_copy(shift, "send").start()
    hist_in.wait()
    halo_v[group] = hist_v[wanted[0, group]]
    for shift in shifts:
        idx_copy(shift, "recv").wait_recv()
        pack_v[slot(shift)] = hist_v[idx[peer(shift), 0, group]]
        halo_copy(shift, "send").start()
    tiles_in.wait()

    zero_tile = jnp.zeros((tile, tile), F32)
    zero_prod = jnp.zeros((tile, ws_v.shape[0]), F32)
    run_tile[0] = zero_tile
    run_prod[0] = zero_prod

    def build(micro, carry):
        total = zero_tile
        for t in range(count):
            total = total + tiles_v[micro * count + table[micro, t]].astype(F32)
            run_tile[t + 1] = total
        for b in range(blocks):
            for s in range(blocks):
                at = 2 * count + b * (blocks + 1) + s
                cell = run_tile[table[micro, at + 1]] - run_tile[table[micro, at]]
                dense_v[micro, b * tile : (b + 1) * tile, s * tile : (s + 1) * tile] = cell.astype(BF16)
        return carry

    lax.fori_loop(0, micros, build, 0)

    for shift in shifts:
        halo_copy(shift, "recv").wait_recv()

    def far(micro):
        total = zero_prod
        for t in range(count):
            total = total + jnp.dot(
                tiles_v[micro * count + table[micro, t]],
                halo_v[table[micro, count + t]],
                preferred_element_type=F32,
            )
            run_prod[t + 1] = total
        for b in range(blocks):
            at = 2 * count + b * (blocks + 1) + blocks
            agg_v[b * tile : (b + 1) * tile] = run_prod[table[micro, at + 1]] - run_prod[table[micro, at]]

    def hop(micro, part):
        at = pl.ds(micro * rows + part * half, half)
        return pltpu.make_async_remote_copy(
            src_ref=out_v.at[at],
            dst_ref=cur_v.at[at],
            send_sem=hop_send.at[micro, part],
            recv_sem=hop_recv.at[micro, part],
            device_id={"section": jnp.minimum(section + 1, last)},
            device_id_type=MESH,
        )

    def emb_copy(micro, to):
        return pltpu.make_async_remote_copy(
            src_ref=turn_v.at[micro, pl.ds(to * share, share)],
            dst_ref=emb.at[:, pl.ds(micro * rows, rows)],
            send_sem=emb_send.at[micro, to],
            recv_sem=emb_recv.at[micro],
            device_id={"section": to},
            device_id_type=MESH,
        )

    def emb_own(micro):
        return pltpu.make_async_copy(
            turn_v.at[micro, pl.ds(last * share, share)],
            emb.at[:, pl.ds(micro * rows, rows)],
            own_sem.at[micro],
        )

    def keep(micro):
        at = pl.ds(micro * rows, rows)
        return pltpu.make_async_copy(cur_v.at[at], fresh.at[at], fresh_sem.at[micro])

    ws_in.wait()
    wn_in.wait()

    @pl.when(section == 0)
    def _():
        feat_in.wait()

    far(0)

    def advance(micro, carry):
        @pl.when(section > 0)
        def _():
            hop(micro, 0).wait_recv()
            hop(micro, 1).wait_recv()

        keep(micro).start()
        inputs = cur_v[pl.ds(micro * rows, rows)]
        for part in range(2):
            own = cur_v[pl.ds(micro * rows + part * half, half)]
            near = jnp.dot(dense_v[micro, part * half : (part + 1) * half], inputs, preferred_element_type=F32)
            aggregate = (agg_v[part * half : (part + 1) * half] + near).astype(BF16)
            pre = jnp.dot(own, ws_v[...], preferred_element_type=F32)
            pre = pre + jnp.dot(aggregate, wn_v[...], preferred_element_type=F32) + bias[...]
            center = pre - jnp.mean(pre, axis=1, keepdims=True)
            variance = jnp.mean(center * center, axis=1, keepdims=True)
            normed = center * lax.rsqrt(variance + 1e-05) * gain[...]
            result = own.astype(F32) + jnp.maximum(normed, 0.0)
            out_v[pl.ds(micro * rows + part * half, half)] = result.astype(BF16)

            @pl.when(section < last)
            def _():
                hop(micro, part).start()

            @pl.when(section == last)
            def _():
                turn_v[micro, :, part * half : (part + 1) * half] = result.T.astype(BF16)

        @pl.when(section == last)
        def _():
            for to in range(last):
                emb_copy(micro, to).start()
            emb_own(micro).start()

        @pl.when(micro < micros - 1)
        def _():
            far(micro + 1)

        return carry

    lax.fori_loop(0, micros, advance, 0)

    for shift in shifts:
        idx_copy(shift, "send").wait_send()
        halo_copy(shift, "send").wait_send()

    def finish(micro, carry):
        keep(micro).wait()

        @pl.when(section < last)
        def _():
            hop(micro, 0).wait_send()
            hop(micro, 1).wait_send()
            emb_copy(micro, 0).wait_recv()

        @pl.when(section == last)
        def _():
            for to in range(last):
                emb_copy(micro, to).wait_send()
            emb_own(micro).wait()

        return carry

    lax.fori_loop(0, micros, finish, 0)


def per_device(
    features, history, halo_blocks, tile_values, tile_dst, tile_src, w_self, w_neigh, bias, gain
):
    sections = lax.axis_size("section")
    groups = lax.axis_size("group")
    nodes, width = features.shape
    micros, count, tile = tile_values.shape[:3]
    rows = nodes // micros
    blocks = rows // tile
    share = width // sections
    table = tile_table(tile_dst, tile_src, blocks, blocks + groups)
    smem = pl.BlockSpec(memory_space=pltpu.SMEM)
    vmem = pl.BlockSpec(memory_space=pltpu.VMEM)
    hbm = pl.BlockSpec(memory_space=pl.ANY)
    emb, fresh = pl.pallas_call(
        kernel,
        out_shape=(
            jax.ShapeDtypeStruct((share, nodes), BF16),
            jax.ShapeDtypeStruct((nodes, width), BF16),
        ),
        in_specs=[smem, smem, hbm, hbm, hbm, hbm, hbm, vmem, vmem],
        out_specs=(hbm, hbm),
        scratch_shapes=[
            pltpu.SMEM((groups, 1, groups), jnp.int32),
            pltpu.VMEM((nodes // tile, tile, width), BF16),
            pltpu.VMEM((micros * count, tile, tile), BF16),
            pltpu.VMEM((groups, tile, width), BF16),
            pltpu.VMEM((groups, tile, width), BF16),
            pltpu.VMEM((micros, rows, rows), BF16),
            pltpu.VMEM((count + 1, tile, tile), F32),
            pltpu.VMEM((count + 1, tile, width), F32),
            pltpu.VMEM((rows, width), F32),
            pltpu.VMEM((nodes, width), BF16),
            pltpu.VMEM((nodes, width), BF16),
            pltpu.VMEM((micros, width, rows), BF16),
            pltpu.VMEM((width, width), BF16),
            pltpu.VMEM((width, width), BF16),
            pltpu.SemaphoreType.DMA((5,)),
            pltpu.SemaphoreType.DMA((micros,)),
            pltpu.SemaphoreType.DMA((micros,)),
            pltpu.SemaphoreType.DMA((groups,)),
            pltpu.SemaphoreType.DMA((groups,)),
            pltpu.SemaphoreType.DMA((groups,)),
            pltpu.SemaphoreType.DMA((groups,)),
            pltpu.SemaphoreType.DMA((micros, 2)),
            pltpu.SemaphoreType.DMA((micros, 2)),
            pltpu.SemaphoreType.DMA((micros, sections)),
            pltpu.SemaphoreType.DMA((micros,)),
        ],
        compiler_params=pltpu.CompilerParams(
            collective_id=0, has_side_effects=True, vmem_limit_bytes=52 * 1024 * 1024
        ),
    )(
        table,
        halo_blocks.reshape(1, groups),
        features,
        history.reshape(nodes // tile, tile, width),
        tile_values.reshape(micros * count, tile, tile),
        w_self[0],
        w_neigh[0],
        bias,
        gain,
    )
    return emb.T, fresh.reshape(1, nodes, width)


def solution(mesh):
    placed = (
        P("group", None),
        P("section", "group", None),
        P("group", None, None),
        P("group", None, None, None),
        P("group", None),
        P("group", None),
        P("section", None, None),
        P("section", None, None),
        P("section", None),
        P("section", None),
    )
    return jax.shard_map(
        per_device,
        mesh=mesh,
        in_specs=placed,
        out_specs=(P("group", "section"), P("section", "group", None)),
        check_vma=False,
    )
```

```python
import functools

import jax
import jax.numpy as jnp
from jax import lax
from jax.experimental import pallas as pl
from jax.experimental.pallas import tpu as pltpu
from jax.sharding import PartitionSpec as P

MESH = pl.DeviceIdType.MESH
F32 = jnp.float32
BF16 = jnp.bfloat16
SIDE = 4


def tile_table(targets, sources, blocks, span):
    micros, count = targets.shape
    key = targets * span + sources
    far_source = jnp.maximum(sources - blocks, 0)
    at = lax.broadcasted_iota(jnp.int32, (micros, count), 1)
    rank = jnp.zeros((micros, count), jnp.int32)
    for j in range(count):
        other = key[:, j : j + 1]
        rank = rank + jnp.where((other < key) | ((other == key) & (at > j)), 1, 0)
    lane = lax.broadcasted_iota(jnp.int32, (micros, 128), 1)
    place = jnp.where(lane < count, lane, lane - count)
    cell = lane - 2 * count
    block = sum(jnp.where(cell >= b * (blocks + 1), 1, 0) for b in range(1, blocks + 1))
    limit = block * span + cell - block * (blocks + 1)
    table = jnp.zeros((micros, 128), jnp.int32)
    for t in range(count):
        chosen = jnp.where(lane < count, t, far_source[:, t : t + 1])
        sorted_part = jnp.where(rank[:, t : t + 1] == place, chosen, 0)
        start_part = jnp.where(key[:, t : t + 1] < limit, 1, 0)
        table = table + jnp.where(lane < 2 * count, sorted_part, start_part)
    return table


def kernel(
    wanted,
    targets,
    sources,
    features,
    history,
    tiles,
    weight_self,
    weight_neigh,
    bias,
    gain,
    emb,
    fresh,
    idx,
    own_idx,
    table,
    table_v,
    dst_v,
    src_v,
    hist_v,
    tiles_v,
    halo_v,
    pack_v,
    dense_v,
    run_tile,
    run_prod,
    agg_v,
    stage_v,
    cur_v,
    mid_v,
    out_v,
    turn_v,
    ws_v,
    wn_v,
    bias_v,
    gain_v,
    local_sem,
    keep_sem,
    own_sem,
    idx_send,
    idx_recv,
    halo_send,
    halo_recv,
    hop_send,
    hop_recv,
    emb_send,
    emb_recv,
    pair_send,
    pair_recv,
    agg_send,
    agg_recv,
    give_send,
    give_recv,
):
    section = lax.axis_index("section")
    group = lax.axis_index("group")
    sections = lax.axis_size("section")
    groups = lax.axis_size("group")
    side = section % 2
    sibling = section + 1 - 2 * side
    first = section < 2
    top = section >= sections - 2
    micros = dense_v.shape[0]
    each = micros // 2
    count = tiles_v.shape[0] // micros
    rows = dense_v.shape[1]
    half = rows // 2
    tile = tiles_v.shape[1]
    blocks = rows // tile
    share = emb.shape[0]
    gx, gy = group // SIDE, group % SIDE
    shifts = [(dx, dy) for dx in range(SIDE) for dy in range(SIDE) if dx or dy]

    def peer(shift):
        return ((gx + shift[0]) % SIDE) * SIDE + (gy + shift[1]) % SIDE

    def slot(shift):
        return shift[0] * SIDE + shift[1]

    def back(shift):
        return ((-shift[0]) % SIDE, (-shift[1]) % SIDE)

    wanted_in = pltpu.make_async_copy(wanted, own_idx, local_sem.at[0])
    dst_in = pltpu.make_async_copy(targets, dst_v, local_sem.at[1])
    src_in = pltpu.make_async_copy(sources, src_v, local_sem.at[2])
    hist_in = pltpu.make_async_copy(history, hist_v, local_sem.at[3])
    feat_in = pltpu.make_async_copy(features, cur_v, local_sem.at[4])
    tiles_in = pltpu.make_async_copy(tiles, tiles_v, local_sem.at[5])
    params = [(weight_self, ws_v), (weight_neigh, wn_v), (bias, bias_v), (gain, gain_v)]
    params_in = [
        pltpu.make_async_copy(source, target.at[side], local_sem.at[6 + i])
        for i, (source, target) in enumerate(params)
    ]
    for copy in [wanted_in, dst_in, src_in, hist_in] + params_in:
        copy.start()

    @pl.when(section == 0)
    def _():
        feat_in.start()

    tiles_in.start()

    barrier = pltpu.get_barrier_semaphore()
    for shift in shifts:
        pl.semaphore_signal(barrier, inc=1, device_id={"group": peer(shift)}, device_id_type=MESH)
    for step in range(1, sections):
        pl.semaphore_signal(
            barrier, inc=1, device_id={"section": (section + step) % sections}, device_id_type=MESH
        )

    dst_in.wait()
    src_in.wait()
    table_v[...] = tile_table(dst_v[...], src_v[...], blocks, blocks + groups)
    table_in = pltpu.make_async_copy(table_v, table, local_sem.at[10])
    table_in.start()
    wanted_in.wait()
    pl.semaphore_wait(barrier, groups + sections - 2)

    def idx_copy(shift, way):
        return pltpu.make_async_remote_copy(
            src_ref=own_idx,
            dst_ref=idx.at[group if way == "send" else peer(shift)],
            send_sem=idx_send.at[slot(shift)],
            recv_sem=idx_recv.at[slot(shift if way == "send" else back(shift))],
            device_id={"group": peer(shift)},
            device_id_type=MESH,
        )

    def halo_copy(shift, way):
        return pltpu.make_async_remote_copy(
            src_ref=pack_v.at[slot(shift)],
            dst_ref=halo_v.at[group if way == "send" else peer(shift)],
            send_sem=halo_send.at[slot(shift)],
            recv_sem=halo_recv.at[slot(shift if way == "send" else back(shift))],
            device_id={"group": peer(shift)},
            device_id_type=MESH,
        )

    params_out = [
        pltpu.make_async_remote_copy(
            src_ref=source,
            dst_ref=target.at[side],
            send_sem=pair_send.at[i],
            recv_sem=pair_recv.at[i],
            device_id={"section": sibling},
            device_id_type=MESH,
        )
        for i, (source, target) in enumerate(params)
    ]

    for shift in shifts:
        idx_copy(shift, "send").start()
    hist_in.wait()
    halo_v[group] = hist_v[own_idx[0, group]]
    for shift in shifts:
        idx_copy(shift, "recv").wait_recv()
        pack_v[slot(shift)] = hist_v[idx[peer(shift), 0, group]]
        halo_copy(shift, "send").start()
    for copy in params_out:
        copy.start()
    tiles_in.wait()
    table_in.wait()

    zero_tile = jnp.zeros((tile, tile), F32)
    zero_prod = jnp.zeros((tile, ws_v.shape[1]), F32)
    run_tile[0] = zero_tile
    run_prod[0] = zero_prod

    def build(micro, carry):
        total = zero_tile
        for t in range(count):
            total = total + tiles_v[micro * count + table[micro, t]].astype(F32)
            run_tile[t + 1] = total
        for b in range(blocks):
            for s in range(blocks):
                at = 2 * count + b * (blocks + 1) + s
                cell = run_tile[table[micro, at + 1]] - run_tile[table[micro, at]]
                dense_v[micro, b * tile : (b + 1) * tile, s * tile : (s + 1) * tile] = cell.astype(BF16)
        return carry

    lax.fori_loop(0, micros, build, 0)

    for shift in shifts:
        halo_copy(shift, "recv").wait_recv()

    def far(micro, result):
        total = zero_prod
        for t in range(count):
            total = total + jnp.dot(
                tiles_v[micro * count + table[micro, t]],
                halo_v[table[micro, count + t]],
                preferred_element_type=F32,
            )
            run_prod[t + 1] = total
        for b in range(blocks):
            at = 2 * count + b * (blocks + 1) + blocks
            result[b * tile : (b + 1) * tile] = run_prod[table[micro, at + 1]] - run_prod[table[micro, at]]

    def layer(micro, source, near_from, result, step, part):
        at = pl.ds(micro * rows + part * half, half)
        own = source[at]
        near = jnp.dot(
            dense_v[micro, part * half : (part + 1) * half],
            source[pl.ds(micro * rows, rows)],
            preferred_element_type=F32,
        )
        aggregate = (near_from[part * half : (part + 1) * half] + near).astype(BF16)
        pre = jnp.dot(own, ws_v[step], preferred_element_type=F32)
        pre = pre + jnp.dot(aggregate, wn_v[step], preferred_element_type=F32) + bias_v[step]
        center = pre - jnp.mean(pre, axis=1, keepdims=True)
        variance = jnp.mean(center * center, axis=1, keepdims=True)
        normed = center * lax.rsqrt(variance + 1e-05) * gain_v[step]
        value = own.astype(F32) + jnp.maximum(normed, 0.0)
        if result is not None:
            result[at] = value.astype(BF16)
        return value

    def hop(micro, part):
        at = pl.ds(micro * rows + part * half, half)
        onward = jnp.where(section == 0, 1, jnp.where(section == 1, 2 + micro % 2, section + 2))
        return pltpu.make_async_remote_copy(
            src_ref=out_v.at[at],
            dst_ref=cur_v.at[at],
            send_sem=hop_send.at[micro, part],
            recv_sem=hop_recv.at[micro, part],
            device_id={"section": onward % sections},
            device_id_type=MESH,
        )

    def emb_copy(micro, step):
        to = (section + step) % sections
        return pltpu.make_async_remote_copy(
            src_ref=turn_v.at[micro, pl.ds(to * share, share)],
            dst_ref=emb.at[:, pl.ds(micro * rows, rows)],
            send_sem=emb_send.at[micro, step],
            recv_sem=emb_recv.at[micro],
            device_id={"section": to},
            device_id_type=MESH,
        )

    def emb_own(micro):
        return pltpu.make_async_copy(
            turn_v.at[micro, pl.ds(section * share, share)],
            emb.at[:, pl.ds(micro * rows, rows)],
            own_sem.at[micro],
        )

    def keep(micro, source):
        at = pl.ds(micro * rows, rows)
        return pltpu.make_async_copy(source.at[at], fresh.at[at], keep_sem.at[micro])

    def give(micro, source):
        at = pl.ds(micro * rows, rows)
        return pltpu.make_async_remote_copy(
            src_ref=source.at[at],
            dst_ref=fresh.at[at],
            send_sem=give_send.at[micro],
            recv_sem=give_recv.at[micro],
            device_id={"section": sibling},
            device_id_type=MESH,
        )

    def agg_copy(j):
        return pltpu.make_async_remote_copy(
            src_ref=stage_v.at[j],
            dst_ref=agg_v.at[side, j],
            send_sem=agg_send.at[j],
            recv_sem=agg_recv.at[j],
            device_id={"section": sibling},
            device_id_type=MESH,
        )

    for copy in params_in:
        copy.wait()

    @pl.when(first)
    def _():
        @pl.when(section == 0)
        def _():
            feat_in.wait()

        far(0, agg_v.at[0, 0])

        def advance(micro, carry):
            @pl.when(section > 0)
            def _():
                hop(micro, 0).wait_recv()
                hop(micro, 1).wait_recv()

            keep(micro, cur_v).start()
            for part in range(2):
                layer(micro, cur_v, agg_v.at[0, 0], out_v, side, part)
                hop(micro, part).start()

            @pl.when(micro < micros - 1)
            def _():
                far(micro + 1, agg_v.at[0, 0])

            return carry

        lax.fori_loop(0, micros, advance, 0)

    @pl.when(jnp.logical_not(first))
    def _():
        def prepare(j, carry):
            far(2 * j + 1 - side, stage_v.at[j])
            agg_copy(j).start()
            far(2 * j + side, agg_v.at[side, j])
            return carry

        lax.fori_loop(0, each, prepare, 0)
        for copy in params_out:
            copy.wait_recv()

        def advance(j, carry):
            micro = 2 * j + side
            agg_copy(j).wait_recv()
            hop(micro, 0).wait_recv()
            hop(micro, 1).wait_recv()
            for part in range(2):
                layer(micro, cur_v, agg_v.at[0, j], mid_v, 0, part)
            for part in range(2):
                value = layer(micro, mid_v, agg_v.at[1, j], out_v, 1, part)

                @pl.when(top)
                def _():
                    turn_v[micro, :, part * half : (part + 1) * half] = value.T.astype(BF16)

                @pl.when(jnp.logical_not(top))
                def _():
                    hop(micro, part).start()

            @pl.when(top)
            def _():
                for step in range(1, sections):
                    emb_copy(micro, step).start()
                emb_own(micro).start()

            @pl.when(side == 0)
            def _():
                keep(micro, cur_v).start()
                give(micro, mid_v).start()

            @pl.when(side == 1)
            def _():
                keep(micro, mid_v).start()
                give(micro, cur_v).start()

            return carry

        lax.fori_loop(0, each, advance, 0)

    for shift in shifts:
        idx_copy(shift, "send").wait_send()
        halo_copy(shift, "send").wait_send()
    for copy in params_out:
        copy.wait_send()

    @pl.when(first)
    def _():
        for copy in params_out:
            copy.wait_recv()

        def finish(micro, carry):
            keep(micro, cur_v).wait()
            hop(micro, 0).wait_send()
            hop(micro, 1).wait_send()
            return carry

        lax.fori_loop(0, micros, finish, 0)

    @pl.when(jnp.logical_not(first))
    def _():
        def finish(j, carry):
            micro = 2 * j + side
            agg_copy(j).wait_send()
            keep(micro, cur_v).wait()
            give(micro, cur_v).wait_send()
            give(2 * j + 1 - side, cur_v).wait_recv()

            @pl.when(jnp.logical_not(top))
            def _():
                hop(micro, 0).wait_send()
                hop(micro, 1).wait_send()

            @pl.when(top)
            def _():
                for step in range(1, sections):
                    emb_copy(micro, step).wait_send()
                emb_own(micro).wait()

            return carry

        lax.fori_loop(0, each, finish, 0)

    def collect(micro, carry):
        @pl.when(section != sections - 2 + micro % 2)
        def _():
            emb_copy(micro, 1).wait_recv()

        return carry

    lax.fori_loop(0, micros, collect, 0)


def per_device(
    features, history, halo_blocks, tile_values, tile_dst, tile_src, w_self, w_neigh, bias, gain
):
    sections = lax.axis_size("section")
    groups = lax.axis_size("group")
    nodes, width = features.shape
    micros, count, tile = tile_values.shape[:3]
    rows = nodes // micros
    share = width // sections
    dma = pltpu.SemaphoreType.DMA
    hbm = pl.BlockSpec(memory_space=pltpu.HBM)
    vmem = pl.BlockSpec(memory_space=pltpu.VMEM)
    emb, fresh = pl.pallas_call(
        kernel,
        out_shape=(
            pltpu.VMEM((share, nodes), BF16),
            pltpu.VMEM((nodes, width), BF16),
        ),
        in_specs=[hbm] * 10,
        out_specs=(vmem, vmem),
        scratch_shapes=[
            pltpu.SMEM((groups, 1, groups), jnp.int32),
            pltpu.SMEM((1, groups), jnp.int32),
            pltpu.SMEM((micros, 128), jnp.int32),
            pltpu.VMEM((micros, 128), jnp.int32),
            pltpu.VMEM((micros, count), jnp.int32),
            pltpu.VMEM((micros, count), jnp.int32),
            pltpu.VMEM((nodes // tile, tile, width), BF16),
            pltpu.VMEM((micros * count, tile, tile), BF16),
            pltpu.VMEM((groups, tile, width), BF16),
            pltpu.VMEM((groups, tile, width), BF16),
            pltpu.VMEM((micros, rows, rows), BF16),
            pltpu.VMEM((count + 1, tile, tile), F32),
            pltpu.VMEM((count + 1, tile, width), F32),
            pltpu.VMEM((2, micros // 2, rows, width), F32),
            pltpu.VMEM((micros // 2, rows, width), F32),
            pltpu.VMEM((nodes, width), BF16),
            pltpu.VMEM((nodes, width), BF16),
            pltpu.VMEM((nodes, width), BF16),
            pltpu.VMEM((micros, width, rows), BF16),
            pltpu.VMEM((2, width, width), BF16),
            pltpu.VMEM((2, width, width), BF16),
            pltpu.VMEM((2, 1, width), F32),
            pltpu.VMEM((2, 1, width), F32),
            dma((11,)),
            dma((micros,)),
            dma((micros,)),
            dma((groups,)),
            dma((groups,)),
            dma((groups,)),
            dma((groups,)),
            dma((micros, 2)),
            dma((micros, 2)),
            dma((micros, sections)),
            dma((micros,)),
            dma((4,)),
            dma((4,)),
            dma((micros // 2,)),
            dma((micros // 2,)),
            dma((micros,)),
            dma((micros,)),
        ],
        compiler_params=pltpu.CompilerParams(
            collective_id=0, has_side_effects=True, vmem_limit_bytes=60 * 1024 * 1024
        ),
    )(
        halo_blocks.reshape(1, groups),
        tile_dst,
        tile_src,
        features,
        history.reshape(nodes // tile, tile, width),
        tile_values.reshape(micros * count, tile, tile),
        w_self[0],
        w_neigh[0],
        bias,
        gain,
    )
    return emb.T, fresh.reshape(1, nodes, width)


def solution(mesh):
    placed = (
        P("group", None),
        P("section", "group", None),
        P("group", None, None),
        P("group", None, None, None),
        P("group", None),
        P("group", None),
        P("section", None, None),
        P("section", None, None),
        P("section", None),
        P("section", None),
    )
    return jax.shard_map(
        per_device,
        mesh=mesh,
        in_specs=placed,
        out_specs=(P("group", "section"), P("section", "group", None)),
        check_vma=False,
    )
```

```python
import functools

import jax
import jax.numpy as jnp
from jax import lax
from jax.experimental import pallas as pl
from jax.experimental.pallas import tpu as pltpu
from jax.sharding import PartitionSpec as P

MESH = pl.DeviceIdType.MESH
F32 = jnp.float32
BF16 = jnp.bfloat16
SIDE = 4
ALONE = ((6, 0), (7, 6))


def tile_table(targets, sources, blocks, span):
    micros, count = targets.shape
    key = targets * span + sources
    far_source = jnp.maximum(sources - blocks, 0)
    at = lax.broadcasted_iota(jnp.int32, (micros, count), 1)
    rank = jnp.zeros((micros, count), jnp.int32)
    for j in range(count):
        other = key[:, j : j + 1]
        rank = rank + jnp.where((other < key) | ((other == key) & (at > j)), 1, 0)
    lane = lax.broadcasted_iota(jnp.int32, (micros, 128), 1)
    place = jnp.where(lane < count, lane, lane - count)
    cell = lane - 2 * count
    block = sum(jnp.where(cell >= b * (blocks + 1), 1, 0) for b in range(1, blocks + 1))
    limit = block * span + cell - block * (blocks + 1)
    table = jnp.zeros((micros, 128), jnp.int32)
    for t in range(count):
        chosen = jnp.where(lane < count, t, far_source[:, t : t + 1])
        sorted_part = jnp.where(rank[:, t : t + 1] == place, chosen, 0)
        start_part = jnp.where(key[:, t : t + 1] < limit, 1, 0)
        table = table + jnp.where(lane < 2 * count, sorted_part, start_part)
    return table


def kernel(
    wanted,
    targets,
    sources,
    features,
    history,
    tiles,
    weight_self,
    weight_neigh,
    bias,
    gain,
    emb,
    fresh,
    idx,
    own_idx,
    table,
    table_v,
    dst_v,
    src_v,
    hist_v,
    tiles_v,
    halo_v,
    pack_v,
    dense_v,
    run_tile,
    run_prod,
    agg_v,
    stage_v,
    cur_v,
    mid_v,
    out_v,
    turn_v,
    ws_v,
    wn_v,
    bias_v,
    gain_v,
    local_sem,
    keep_sem,
    own_sem,
    idx_send,
    idx_recv,
    halo_send,
    halo_recv,
    hop_send,
    hop_recv,
    emb_send,
    emb_recv,
    pair_send,
    pair_recv,
    agg_send,
    agg_recv,
    give_send,
    give_recv,
    zx_v,
    zagg_v,
    zstage_v,
    zws_v,
    zwn_v,
    zbias_v,
    zgain_v,
    zlocal,
    zw_send,
    zw_recv,
    zagg_send,
    zagg_recv,
    zgive_send,
    zgive_recv,
    clear_sem,
):
    section = lax.axis_index("section")
    group = lax.axis_index("group")
    sections = lax.axis_size("section")
    groups = lax.axis_size("group")
    last = sections - 1
    side = section % 2
    sibling = section + 1 - 2 * side
    first = section < 2
    top = section >= sections - 2
    micros = dense_v.shape[0]
    relayed = micros - len(ALONE)
    each = relayed // 2
    owner = functools.reduce(jnp.logical_or, [section == device for _, device in ALONE])
    mine = sum(jnp.where(section == device, z, 0) for z, (_, device) in enumerate(ALONE))
    sole = sum(jnp.where(section == device, micro, 0) for micro, device in ALONE)
    count = tiles_v.shape[0] // micros
    rows = dense_v.shape[1]
    half = rows // 2
    tile = tiles_v.shape[1]
    blocks = rows // tile
    share = emb.shape[0]
    gx, gy = group // SIDE, group % SIDE
    shifts = [(dx, dy) for dx in range(SIDE) for dy in range(SIDE) if dx or dy]

    def peer(shift):
        return ((gx + shift[0]) % SIDE) * SIDE + (gy + shift[1]) % SIDE

    def slot(shift):
        return shift[0] * SIDE + shift[1]

    def back(shift):
        return ((-shift[0]) % SIDE, (-shift[1]) % SIDE)

    wanted_in = pltpu.make_async_copy(wanted, own_idx, local_sem.at[0])
    dst_in = pltpu.make_async_copy(targets, dst_v, local_sem.at[1])
    src_in = pltpu.make_async_copy(sources, src_v, local_sem.at[2])
    hist_in = pltpu.make_async_copy(history, hist_v, local_sem.at[3])
    feat_in = pltpu.make_async_copy(features, cur_v, local_sem.at[4])
    tiles_in = pltpu.make_async_copy(tiles, tiles_v, local_sem.at[5])
    params = [(weight_self, ws_v), (weight_neigh, wn_v), (bias, bias_v), (gain, gain_v)]
    params_in = [
        pltpu.make_async_copy(source, target.at[side], local_sem.at[6 + i])
        for i, (source, target) in enumerate(params)
    ]
    for copy in [wanted_in, dst_in, src_in, hist_in] + params_in:
        copy.start()

    @pl.when(section == 0)
    def _():
        feat_in.start()

    tiles_in.start()
    zparams = [(weight_self, zws_v), (weight_neigh, zwn_v), (bias, zbias_v), (gain, zgain_v)]
    zlocal_in = [
        pltpu.make_async_copy(source, target.at[section], zlocal.at[i])
        for i, (source, target) in enumerate(zparams)
    ] + [pltpu.make_async_copy(features.at[pl.ds(sole * rows, rows)], zx_v.at[0], zlocal.at[4])]

    @pl.when(owner)
    def _():
        for copy in zlocal_in:
            copy.start()

    barrier = pltpu.get_barrier_semaphore()
    for shift in shifts:
        pl.semaphore_signal(barrier, inc=1, device_id={"group": peer(shift)}, device_id_type=MESH)
    for step in range(1, sections):
        pl.semaphore_signal(
            barrier, inc=1, device_id={"section": (section + step) % sections}, device_id_type=MESH
        )

    dst_in.wait()
    src_in.wait()
    table_v[...] = tile_table(dst_v[...], src_v[...], blocks, blocks + groups)
    table_in = pltpu.make_async_copy(table_v, table, local_sem.at[10])
    table_in.start()
    wanted_in.wait()
    pl.semaphore_wait(barrier, groups + sections - 2)

    def idx_copy(shift, way):
        return pltpu.make_async_remote_copy(
            src_ref=own_idx,
            dst_ref=idx.at[group if way == "send" else peer(shift)],
            send_sem=idx_send.at[slot(shift)],
            recv_sem=idx_recv.at[slot(shift if way == "send" else back(shift))],
            device_id={"group": peer(shift)},
            device_id_type=MESH,
        )

    def halo_copy(shift, way):
        return pltpu.make_async_remote_copy(
            src_ref=pack_v.at[slot(shift)],
            dst_ref=halo_v.at[group if way == "send" else peer(shift)],
            send_sem=halo_send.at[slot(shift)],
            recv_sem=halo_recv.at[slot(shift if way == "send" else back(shift))],
            device_id={"group": peer(shift)},
            device_id_type=MESH,
        )

    params_out = [
        pltpu.make_async_remote_copy(
            src_ref=source,
            dst_ref=target.at[side],
            send_sem=pair_send.at[i],
            recv_sem=pair_recv.at[i],
            device_id={"section": sibling},
            device_id_type=MESH,
        )
        for i, (source, target) in enumerate(params)
    ]

    def zparam_copy(z, at, i):
        source, target = zparams[i]
        return pltpu.make_async_remote_copy(
            src_ref=source,
            dst_ref=target.at[at],
            send_sem=zw_send.at[z, i],
            recv_sem=zw_recv.at[at, i],
            device_id={"section": ALONE[z][1]},
            device_id_type=MESH,
        )

    def zagg_copy(z, at):
        return pltpu.make_async_remote_copy(
            src_ref=zstage_v.at[z],
            dst_ref=zagg_v.at[at],
            send_sem=zagg_send.at[z],
            recv_sem=zagg_recv.at[at],
            device_id={"section": ALONE[z][1]},
            device_id_type=MESH,
        )

    def zgive(to):
        return pltpu.make_async_remote_copy(
            src_ref=zx_v.at[to],
            dst_ref=fresh.at[pl.ds(sole * rows, rows)],
            send_sem=zgive_send.at[to],
            recv_sem=zgive_recv.at[mine],
            device_id={"section": to},
            device_id_type=MESH,
        )

    def zgot(z):
        at = pl.ds(ALONE[z][0] * rows, rows)
        return pltpu.make_async_remote_copy(
            src_ref=fresh.at[at],
            dst_ref=fresh.at[at],
            send_sem=zgive_send.at[0],
            recv_sem=zgive_recv.at[z],
            device_id={"section": ALONE[z][1]},
            device_id_type=MESH,
        )

    def zkeep(to):
        return pltpu.make_async_copy(
            zx_v.at[to], fresh.at[pl.ds(sole * rows, rows)], zlocal.at[5]
        )

    for shift in shifts:
        idx_copy(shift, "send").start()
    hist_in.wait()
    halo_v[group] = hist_v[own_idx[0, group]]
    for shift in shifts:
        idx_copy(shift, "recv").wait_recv()
        pack_v[slot(shift)] = hist_v[idx[peer(shift), 0, group]]
        halo_copy(shift, "send").start()

    @pl.when(jnp.logical_not(first))
    def _():
        for copy in params_out:
            copy.start()

    for z, (_, device) in enumerate(ALONE):

        @pl.when(section != device)
        def _():
            for i in range(len(zparams)):
                zparam_copy(z, section, i).start()

    tiles_in.wait()
    table_in.wait()

    zero_tile = jnp.zeros((tile, tile), F32)
    zero_prod = jnp.zeros((tile, ws_v.shape[1]), F32)
    run_tile[0] = zero_tile
    run_prod[0] = zero_prod

    def build(micro, carry):
        total = zero_tile
        for t in range(count):
            total = total + tiles_v[micro * count + table[micro, t]].astype(F32)
            run_tile[t + 1] = total
        for b in range(blocks):
            for s in range(blocks):
                at = 2 * count + b * (blocks + 1) + s
                cell = run_tile[table[micro, at + 1]] - run_tile[table[micro, at]]
                dense_v[micro, b * tile : (b + 1) * tile, s * tile : (s + 1) * tile] = cell.astype(BF16)
        return carry

    lax.fori_loop(0, micros, build, 0)

    for shift in shifts:
        halo_copy(shift, "recv").wait_recv()

    def far(micro, result):
        total = zero_prod
        for t in range(count):
            total = total + jnp.dot(
                tiles_v[micro * count + table[micro, t]],
                halo_v[table[micro, count + t]],
                preferred_element_type=F32,
            )
            run_prod[t + 1] = total
        for b in range(blocks):
            at = 2 * count + b * (blocks + 1) + blocks
            total = run_prod[table[micro, at + 1]] - run_prod[table[micro, at]]
            result[b * tile : (b + 1) * tile] = total.astype(result.dtype)

    def layer(micro, source, far_sum, ws, wn, offset, scale, part):
        own = source[part * half : (part + 1) * half]
        near = jnp.dot(
            dense_v[micro, part * half : (part + 1) * half], source[...], preferred_element_type=F32
        )
        aggregate = (far_sum[part * half : (part + 1) * half].astype(F32) + near).astype(BF16)
        pre = jnp.dot(own, ws[...], preferred_element_type=F32)
        pre = pre + jnp.dot(aggregate, wn[...], preferred_element_type=F32) + offset[...]
        center = pre - jnp.mean(pre, axis=1, keepdims=True)
        variance = jnp.mean(center * center, axis=1, keepdims=True)
        normed = center * lax.rsqrt(variance + 1e-05) * scale[...]
        return own.astype(F32) + jnp.maximum(normed, 0.0)

    def paired(micro, source, far_sum, step, part):
        return layer(
            micro,
            source.at[pl.ds(micro * rows, rows)],
            far_sum,
            ws_v.at[step],
            wn_v.at[step],
            bias_v.at[step],
            gain_v.at[step],
            part,
        )

    def zfar(z):
        micro, device = ALONE[z]

        @pl.when(section == device)
        def _():
            far(micro, zagg_v.at[section])

        @pl.when(section != device)
        def _():
            far(micro, zstage_v.at[z])
            zagg_copy(z, section).start()

    def alone():
        for copy in zlocal_in:
            copy.wait()

        def climb(depth, carry):
            @pl.when(depth != section)
            def _():
                zagg_copy(0, depth).wait_recv()
                for i in range(len(zparams)):
                    zparam_copy(0, depth, i).wait_recv()

            for part in range(2):
                value = layer(
                    sole,
                    zx_v.at[depth],
                    zagg_v.at[depth],
                    zws_v.at[depth],
                    zwn_v.at[depth],
                    zbias_v.at[depth],
                    zgain_v.at[depth],
                    part,
                )
                zx_v[depth + 1, part * half : (part + 1) * half] = value.astype(BF16)

            @pl.when(jnp.logical_and(depth < last, jnp.logical_and(section > 0, depth + 1 != section)))
            def _():
                zgive(depth + 1).start()

            @pl.when(depth + 1 == section)
            def _():
                zkeep(depth + 1).start()

            return carry

        lax.fori_loop(0, sections, climb, 0)

        @pl.when(section == 0)
        def _():
            pl.semaphore_wait(clear_sem, 1)
            for to in range(1, sections):
                zgive(to).start()

        turn_v[sole] = zx_v[sections].astype(F32).T.astype(BF16)
        for step in range(1, sections):
            emb_copy(sole, step).start()
        emb_own(sole).start()

    def hop(micro, part):
        at = pl.ds(micro * rows + part * half, half)
        onward = jnp.where(section == 0, 1, jnp.where(section == 1, 2 + micro % 2, section + 2))
        return pltpu.make_async_remote_copy(
            src_ref=out_v.at[at],
            dst_ref=cur_v.at[at],
            send_sem=hop_send.at[micro, part],
            recv_sem=hop_recv.at[micro, part],
            device_id={"section": onward % sections},
            device_id_type=MESH,
        )

    def emb_copy(micro, step):
        to = (section + step) % sections
        return pltpu.make_async_remote_copy(
            src_ref=turn_v.at[micro, pl.ds(to * share, share)],
            dst_ref=emb.at[:, pl.ds(micro * rows, rows)],
            send_sem=emb_send.at[micro, step],
            recv_sem=emb_recv.at[micro],
            device_id={"section": to},
            device_id_type=MESH,
        )

    def emb_own(micro):
        return pltpu.make_async_copy(
            turn_v.at[micro, pl.ds(section * share, share)],
            emb.at[:, pl.ds(micro * rows, rows)],
            own_sem.at[micro],
        )

    def keep(micro, source):
        at = pl.ds(micro * rows, rows)
        return pltpu.make_async_copy(source.at[at], fresh.at[at], keep_sem.at[micro])

    def give(micro, source):
        at = pl.ds(micro * rows, rows)
        return pltpu.make_async_remote_copy(
            src_ref=source.at[at],
            dst_ref=fresh.at[at],
            send_sem=give_send.at[micro],
            recv_sem=give_recv.at[micro],
            device_id={"section": sibling},
            device_id_type=MESH,
        )

    def agg_copy(j):
        return pltpu.make_async_remote_copy(
            src_ref=stage_v.at[j],
            dst_ref=agg_v.at[side, j],
            send_sem=agg_send.at[j],
            recv_sem=agg_recv.at[j],
            device_id={"section": sibling},
            device_id_type=MESH,
        )

    for copy in params_in:
        copy.wait()

    @pl.when(first)
    def _():
        @pl.when(section == 0)
        def _():
            feat_in.wait()

        far(0, agg_v.at[0, 0])

        def advance(micro, carry):
            @pl.when(section > 0)
            def _():
                hop(micro, 0).wait_recv()
                hop(micro, 1).wait_recv()

            keep(micro, cur_v).start()
            for part in range(2):
                value = paired(micro, cur_v, agg_v.at[0, 0], side, part)
                out_v[pl.ds(micro * rows + part * half, half)] = value.astype(BF16)
                hop(micro, part).start()

            @pl.when(micro < relayed - 1)
            def _():
                far(micro + 1, agg_v.at[0, 0])

            for z in range(len(ALONE)):

                @pl.when(micro == z)
                def _():
                    zfar(z)

            return carry

        lax.fori_loop(0, relayed, advance, 0)

        @pl.when(section == 0)
        def _():
            for micro, _ in ALONE:
                keep(micro, cur_v).start()

        @pl.when(section == 1)
        def _():
            def sent(micro, carry):
                hop(micro, 0).wait_send()
                hop(micro, 1).wait_send()
                return carry

            lax.fori_loop(0, relayed, sent, 0)
            pl.semaphore_signal(clear_sem, inc=1, device_id={"section": sibling}, device_id_type=MESH)

        @pl.when(owner)
        def _():
            alone()

    @pl.when(jnp.logical_not(first))
    def _():
        for z in reversed(range(len(ALONE))):
            zfar(z)

        def prepare(j, carry):
            far(2 * j + 1 - side, stage_v.at[j])
            agg_copy(j).start()
            far(2 * j + side, agg_v.at[side, j])
            return carry

        lax.fori_loop(0, each, prepare, 0)
        for copy in params_out:
            copy.wait_recv()

        @pl.when(owner)
        def _():
            alone()

        def advance(j, carry):
            micro = 2 * j + side
            agg_copy(j).wait_recv()
            hop(micro, 0).wait_recv()
            hop(micro, 1).wait_recv()
            for part in range(2):
                value = paired(micro, cur_v, agg_v.at[0, j], 0, part)
                mid_v[pl.ds(micro * rows + part * half, half)] = value.astype(BF16)
            for part in range(2):
                value = paired(micro, mid_v, agg_v.at[1, j], 1, part)

                @pl.when(top)
                def _():
                    turn_v[micro, :, part * half : (part + 1) * half] = value.T.astype(BF16)

                @pl.when(jnp.logical_not(top))
                def _():
                    out_v[pl.ds(micro * rows + part * half, half)] = value.astype(BF16)
                    hop(micro, part).start()

            @pl.when(top)
            def _():
                for step in range(1, sections):
                    emb_copy(micro, step).start()
                emb_own(micro).start()

            @pl.when(side == 0)
            def _():
                keep(micro, cur_v).start()
                give(micro, mid_v).start()

            @pl.when(side == 1)
            def _():
                keep(micro, mid_v).start()
                give(micro, cur_v).start()

            return carry

        lax.fori_loop(0, each, advance, 0)

    for shift in shifts:
        idx_copy(shift, "send").wait_send()
        halo_copy(shift, "send").wait_send()
    @pl.when(first)
    def _():
        def finish(micro, carry):
            keep(micro, cur_v).wait()

            @pl.when(section == 0)
            def _():
                hop(micro, 0).wait_send()
                hop(micro, 1).wait_send()

            return carry

        lax.fori_loop(0, relayed, finish, 0)

        @pl.when(section == 0)
        def _():
            for micro, _ in ALONE:
                keep(micro, cur_v).wait()

    for z, (_, device) in enumerate(ALONE):

        @pl.when(section != device)
        def _():
            for i in range(len(zparams)):
                zparam_copy(z, section, i).wait_send()
            zagg_copy(z, section).wait_send()

            @pl.when(section > 0)
            def _():
                zgot(z).wait_recv()

    @pl.when(owner)
    def _():
        def given(to, carry):
            @pl.when(to != section)
            def _():
                zgive(to).wait_send()

            @pl.when(to == section)
            def _():
                zkeep(to).wait()

            return carry

        lax.fori_loop(1, sections, given, 0)
        for step in range(1, sections):
            emb_copy(sole, step).wait_send()
        emb_own(sole).wait()

    @pl.when(jnp.logical_not(first))
    def _():
        for copy in params_out:
            copy.wait_send()

        def finish(j, carry):
            micro = 2 * j + side
            agg_copy(j).wait_send()
            keep(micro, cur_v).wait()
            give(micro, cur_v).wait_send()
            give(2 * j + 1 - side, cur_v).wait_recv()

            @pl.when(jnp.logical_not(top))
            def _():
                hop(micro, 0).wait_send()
                hop(micro, 1).wait_send()

            @pl.when(top)
            def _():
                for step in range(1, sections):
                    emb_copy(micro, step).wait_send()
                emb_own(micro).wait()

            return carry

        lax.fori_loop(0, each, finish, 0)

    def collect(micro, carry):
        @pl.when(section != sections - 2 + micro % 2)
        def _():
            emb_copy(micro, 1).wait_recv()

        return carry

    lax.fori_loop(0, relayed, collect, 0)
    for micro, device in ALONE:

        @pl.when(section != device)
        def _():
            emb_copy(micro, 1).wait_recv()


def per_device(
    features, history, halo_blocks, tile_values, tile_dst, tile_src, w_self, w_neigh, bias, gain
):
    sections = lax.axis_size("section")
    groups = lax.axis_size("group")
    nodes, width = features.shape
    micros, count, tile = tile_values.shape[:3]
    rows = nodes // micros
    share = width // sections
    dma = pltpu.SemaphoreType.DMA
    hbm = pl.BlockSpec(memory_space=pltpu.HBM)
    vmem = pl.BlockSpec(memory_space=pltpu.VMEM)
    emb, fresh = pl.pallas_call(
        kernel,
        out_shape=(
            pltpu.VMEM((share, nodes), BF16),
            pltpu.VMEM((nodes, width), BF16),
        ),
        in_specs=[hbm] * 10,
        out_specs=(vmem, vmem),
        scratch_shapes=[
            pltpu.SMEM((groups, 1, groups), jnp.int32),
            pltpu.SMEM((1, groups), jnp.int32),
            pltpu.SMEM((micros, 128), jnp.int32),
            pltpu.VMEM((micros, 128), jnp.int32),
            pltpu.VMEM((micros, count), jnp.int32),
            pltpu.VMEM((micros, count), jnp.int32),
            pltpu.VMEM((nodes // tile, tile, width), BF16),
            pltpu.VMEM((micros * count, tile, tile), BF16),
            pltpu.VMEM((groups, tile, width), BF16),
            pltpu.VMEM((groups, tile, width), BF16),
            pltpu.VMEM((micros, rows, rows), BF16),
            pltpu.VMEM((count + 1, tile, tile), F32),
            pltpu.VMEM((count + 1, tile, width), F32),
            pltpu.VMEM((2, micros // 2, rows, width), F32),
            pltpu.VMEM((micros // 2, rows, width), F32),
            pltpu.VMEM((nodes, width), BF16),
            pltpu.VMEM((nodes, width), BF16),
            pltpu.VMEM((nodes, width), BF16),
            pltpu.VMEM((micros, width, rows), BF16),
            pltpu.VMEM((2, width, width), BF16),
            pltpu.VMEM((2, width, width), BF16),
            pltpu.VMEM((2, 1, width), F32),
            pltpu.VMEM((2, 1, width), F32),
            dma((11,)),
            dma((micros,)),
            dma((micros,)),
            dma((groups,)),
            dma((groups,)),
            dma((groups,)),
            dma((groups,)),
            dma((micros, 2)),
            dma((micros, 2)),
            dma((micros, sections)),
            dma((micros,)),
            dma((4,)),
            dma((4,)),
            dma((micros // 2,)),
            dma((micros // 2,)),
            dma((micros,)),
            dma((micros,)),
            pltpu.VMEM((sections + 1, rows, width), BF16),
            pltpu.VMEM((sections, rows, width), BF16),
            pltpu.VMEM((len(ALONE), rows, width), BF16),
            pltpu.VMEM((sections, width, width), BF16),
            pltpu.VMEM((sections, width, width), BF16),
            pltpu.VMEM((sections, 1, width), F32),
            pltpu.VMEM((sections, 1, width), F32),
            dma((6,)),
            dma((len(ALONE), 4)),
            dma((sections, 4)),
            dma((len(ALONE),)),
            dma((sections,)),
            dma((sections,)),
            dma((len(ALONE),)),
            pltpu.SemaphoreType.REGULAR,
        ],
        compiler_params=pltpu.CompilerParams(
            collective_id=0, has_side_effects=True, vmem_limit_bytes=60 * 1024 * 1024
        ),
    )(
        halo_blocks.reshape(1, groups),
        tile_dst,
        tile_src,
        features,
        history.reshape(nodes // tile, tile, width),
        tile_values.reshape(micros * count, tile, tile),
        w_self[0],
        w_neigh[0],
        bias,
        gain,
    )
    return emb.T, fresh.reshape(1, nodes, width)


def solution(mesh):
    placed = (
        P("group", None),
        P("section", "group", None),
        P("group", None, None),
        P("group", None, None, None),
        P("group", None),
        P("group", None),
        P("section", None, None),
        P("section", None, None),
        P("section", None),
        P("section", None),
    )
    return jax.shard_map(
        per_device,
        mesh=mesh,
        in_specs=placed,
        out_specs=(P("group", "section"), P("section", "group", None)),
        check_vma=False,
    )
```

```python
import functools

import jax
import jax.numpy as jnp
from jax import lax
from jax.experimental import pallas as pl
from jax.experimental.pallas import tpu as pltpu
from jax.sharding import PartitionSpec as P

MESH = pl.DeviceIdType.MESH
F32 = jnp.float32
BF16 = jnp.bfloat16
SIDE = 4
ORDER = (4, 5, 3, 6, 2, 7, 1)
ALONE = ((6, 6), (7, 0))


def tile_table(targets, sources, blocks, span):
    micros, count = targets.shape
    key = targets * span + sources
    far_source = jnp.maximum(sources - blocks, 0)
    at = lax.broadcasted_iota(jnp.int32, (micros, count), 1)
    rank = jnp.zeros((micros, count), jnp.int32)
    for j in range(count):
        other = key[:, j : j + 1]
        rank = rank + jnp.where((other < key) | ((other == key) & (at > j)), 1, 0)
    lane = lax.broadcasted_iota(jnp.int32, (micros, 128), 1)
    place = jnp.where(lane < count, lane, lane - count)
    cell = lane - 2 * count
    block = sum(jnp.where(cell >= b * (blocks + 1), 1, 0) for b in range(1, blocks + 1))
    limit = block * span + cell - block * (blocks + 1)
    table = jnp.zeros((micros, 128), jnp.int32)
    for t in range(count):
        chosen = jnp.where(lane < count, t, far_source[:, t : t + 1])
        sorted_part = jnp.where(rank[:, t : t + 1] == place, chosen, 0)
        start_part = jnp.where(key[:, t : t + 1] < limit, 1, 0)
        table = table + jnp.where(lane < 2 * count, sorted_part, start_part)
    return table


def kernel(
    wanted,
    targets,
    sources,
    features,
    history,
    tiles,
    weight_self,
    weight_neigh,
    bias,
    gain,
    emb,
    fresh,
    idx,
    own_idx,
    table,
    table_v,
    dst_v,
    src_v,
    hist_v,
    tiles_v,
    halo_v,
    pack_v,
    dense_v,
    run_tile,
    run_prod,
    agg_v,
    stage_v,
    cur_v,
    mid_v,
    out_v,
    turn_v,
    ws_v,
    wn_v,
    bias_v,
    gain_v,
    local_sem,
    keep_sem,
    own_sem,
    idx_send,
    idx_recv,
    halo_send,
    halo_recv,
    hop_send,
    hop_recv,
    emb_send,
    emb_recv,
    pair_send,
    pair_recv,
    agg_send,
    agg_recv,
    give_send,
    give_recv,
    zx_v,
    zagg_v,
    zstage_v,
    zws_v,
    zwn_v,
    zbias_v,
    zgain_v,
    zlocal,
    zw_send,
    zw_recv,
    zagg_send,
    zagg_recv,
    zgive_send,
    zgive_recv,
    zpass_send,
    clear_sem,
):
    section = lax.axis_index("section")
    group = lax.axis_index("group")
    sections = lax.axis_size("section")
    groups = lax.axis_size("group")
    last = sections - 1
    side = section % 2
    sibling = section + 1 - 2 * side
    first = section < 2
    top = section >= sections - 2
    micros = dense_v.shape[0]
    relayed = micros - len(ALONE)
    each = (relayed + 1) // 2
    devices = [device for _, device in ALONE]
    twins = [device for device in devices if device ^ 1 in devices]
    twin = functools.reduce(jnp.logical_or, [section == device for device in twins], section < 0)
    owner = functools.reduce(jnp.logical_or, [section == device for _, device in ALONE])
    mine = sum(jnp.where(section == device, z, 0) for z, (_, device) in enumerate(ALONE))
    sole = sum(jnp.where(section == device, micro, 0) for micro, device in ALONE)
    count = tiles_v.shape[0] // micros
    rows = dense_v.shape[1]
    half = rows // 2
    slab = half // 2
    tile = tiles_v.shape[1]
    blocks = rows // tile
    share = emb.shape[0]
    gx, gy = group // SIDE, group % SIDE
    shifts = [(dx, dy) for dx in range(SIDE) for dy in range(SIDE) if dx or dy]

    def peer(shift):
        return ((gx + shift[0]) % SIDE) * SIDE + (gy + shift[1]) % SIDE

    def slot(shift):
        return shift[0] * SIDE + shift[1]

    def back(shift):
        return ((-shift[0]) % SIDE, (-shift[1]) % SIDE)

    wanted_in = pltpu.make_async_copy(wanted, own_idx, local_sem.at[0])
    dst_in = pltpu.make_async_copy(targets, dst_v, local_sem.at[1])
    src_in = pltpu.make_async_copy(sources, src_v, local_sem.at[2])
    hist_in = pltpu.make_async_copy(history, hist_v, local_sem.at[3])
    feat_in = pltpu.make_async_copy(features, cur_v, local_sem.at[4])
    tiles_in = pltpu.make_async_copy(tiles, tiles_v, local_sem.at[5])
    params = [(weight_self, ws_v), (weight_neigh, wn_v), (bias, bias_v), (gain, gain_v)]
    params_in = [
        pltpu.make_async_copy(source, target.at[side], local_sem.at[6 + i])
        for i, (source, target) in enumerate(params)
    ]
    for copy in [wanted_in, dst_in, src_in, hist_in] + params_in:
        copy.start()

    @pl.when(section == 0)
    def _():
        feat_in.start()

    tiles_in.start()
    zparams = [(ws_v, zws_v), (wn_v, zwn_v), (bias_v, zbias_v), (gain_v, zgain_v)]
    zlocal_in = [
        pltpu.make_async_copy(features.at[pl.ds(sole * rows, rows)], zx_v.at[0], zlocal.at[4])
    ]

    @pl.when(owner)
    def _():
        for copy in zlocal_in:
            copy.start()

    barrier = pltpu.get_barrier_semaphore()
    for shift in shifts:
        pl.semaphore_signal(barrier, inc=1, device_id={"group": peer(shift)}, device_id_type=MESH)
    for step in range(1, sections):
        pl.semaphore_signal(
            barrier, inc=1, device_id={"section": (section + step) % sections}, device_id_type=MESH
        )

    for copy in params_in:
        copy.wait()
    for target in (ws_v, wn_v, bias_v):
        raw = target[side].astype(F32)
        target[side] = (raw - jnp.mean(raw, axis=1, keepdims=True)).astype(target.dtype)

    @pl.when(owner)
    def _():
        for source, target in zparams:
            target[section] = source[side]

    dst_in.wait()
    src_in.wait()
    table_v[...] = tile_table(dst_v[...], src_v[...], blocks, blocks + groups)
    table_in = pltpu.make_async_copy(table_v, table, local_sem.at[10])
    table_in.start()
    wanted_in.wait()
    pl.semaphore_wait(barrier, groups + sections - 2)

    def idx_copy(shift, way):
        return pltpu.make_async_remote_copy(
            src_ref=own_idx,
            dst_ref=idx.at[group if way == "send" else peer(shift)],
            send_sem=idx_send.at[slot(shift)],
            recv_sem=idx_recv.at[slot(shift if way == "send" else back(shift))],
            device_id={"group": peer(shift)},
            device_id_type=MESH,
        )

    def halo_copy(shift, way):
        return pltpu.make_async_remote_copy(
            src_ref=pack_v.at[slot(shift)],
            dst_ref=halo_v.at[group if way == "send" else peer(shift)],
            send_sem=halo_send.at[slot(shift)],
            recv_sem=halo_recv.at[slot(shift if way == "send" else back(shift))],
            device_id={"group": peer(shift)},
            device_id_type=MESH,
        )

    params_out = [
        pltpu.make_async_remote_copy(
            src_ref=target.at[side],
            dst_ref=target.at[side],
            send_sem=pair_send.at[i],
            recv_sem=pair_recv.at[i],
            device_id={"section": sibling},
            device_id_type=MESH,
        )
        for i, (source, target) in enumerate(params)
    ]

    def zparam_copy(z, at, i):
        source, target = zparams[i]
        return pltpu.make_async_remote_copy(
            src_ref=source.at[side],
            dst_ref=target.at[at],
            send_sem=zw_send.at[z, i],
            recv_sem=zw_recv.at[at, i],
            device_id={"section": ALONE[z][1]},
            device_id_type=MESH,
        )

    def zparam_pass(at, i):
        target = zparams[i][1]
        return pltpu.make_async_remote_copy(
            src_ref=target.at[at],
            dst_ref=target.at[at],
            send_sem=zpass_send.at[at, i],
            recv_sem=zw_recv.at[at, i],
            device_id={"section": sibling},
            device_id_type=MESH,
        )

    def direct(device):
        if device not in twins:
            return section != device
        return jnp.logical_and(
            section != device, jnp.logical_or(side == device % 2, section == device ^ 1)
        )

    def zagg_copy(z, at):
        return pltpu.make_async_remote_copy(
            src_ref=zstage_v.at[z],
            dst_ref=zagg_v.at[at],
            send_sem=zagg_send.at[z],
            recv_sem=zagg_recv.at[at],
            device_id={"section": ALONE[z][1]},
            device_id_type=MESH,
        )

    def zgive(to):
        return pltpu.make_async_remote_copy(
            src_ref=zx_v.at[to],
            dst_ref=fresh.at[pl.ds(sole * rows, rows)],
            send_sem=zgive_send.at[to],
            recv_sem=zgive_recv.at[mine],
            device_id={"section": to},
            device_id_type=MESH,
        )

    def zgot(z):
        at = pl.ds(ALONE[z][0] * rows, rows)
        return pltpu.make_async_remote_copy(
            src_ref=fresh.at[at],
            dst_ref=fresh.at[at],
            send_sem=zgive_send.at[0],
            recv_sem=zgive_recv.at[z],
            device_id={"section": ALONE[z][1]},
            device_id_type=MESH,
        )

    def zkeep(to):
        return pltpu.make_async_copy(
            zx_v.at[to], fresh.at[pl.ds(sole * rows, rows)], zlocal.at[5]
        )

    for shift in shifts:
        idx_copy(shift, "send").start()
    hist_in.wait()
    halo_v[group] = hist_v[own_idx[0, group]]
    for shift in shifts:
        idx_copy(shift, "recv").wait_recv()
        pack_v[slot(shift)] = hist_v[idx[peer(shift), 0, group]]
        halo_copy(shift, "send").start()

    @pl.when(jnp.logical_not(first))
    def _():
        for copy in params_out:
            copy.start()

    for z, (_, device) in enumerate(ALONE):

        @pl.when(direct(device))
        def _():
            for i in range(len(zparams)):
                zparam_copy(z, section, i).start()

    tiles_in.wait()
    table_in.wait()

    zero_tile = jnp.zeros((tile, tile), F32)
    zero_prod = jnp.zeros((tile, ws_v.shape[1]), F32)
    run_tile[0] = zero_tile
    run_prod[0] = zero_prod

    def build(micro, carry):
        total = zero_tile
        for t in range(count):
            total = total + tiles_v[micro * count + table[micro, t]].astype(F32)
            run_tile[t + 1] = total
        for b in range(blocks):
            for s in range(blocks):
                at = 2 * count + b * (blocks + 1) + s
                cell = run_tile[table[micro, at + 1]] - run_tile[table[micro, at]]
                dense_v[micro, b * tile : (b + 1) * tile, s * tile : (s + 1) * tile] = cell.astype(BF16)
        return carry

    lax.fori_loop(0, micros, build, 0)

    for shift in shifts:
        halo_copy(shift, "recv").wait_recv()

    def far(micro, result):
        total = zero_prod
        for t in range(count):
            total = total + jnp.dot(
                tiles_v[micro * count + table[micro, t]],
                halo_v[table[micro, count + t]],
                preferred_element_type=F32,
            )
            run_prod[t + 1] = total
        for b in range(blocks):
            at = 2 * count + b * (blocks + 1) + blocks
            total = run_prod[table[micro, at + 1]] - run_prod[table[micro, at]]
            result[b * tile : (b + 1) * tile] = total.astype(result.dtype)

    def layer(micro, source, far_sum, ws, wn, offset, scale, at):
        own = source[at * slab : (at + 1) * slab]
        near = jnp.dot(
            dense_v[micro, at * slab : (at + 1) * slab], source[...], preferred_element_type=F32
        )
        aggregate = (far_sum[at * slab : (at + 1) * slab].astype(F32) + near).astype(BF16)
        pre = jnp.dot(own, ws[...], preferred_element_type=F32)
        pre = pre + jnp.dot(aggregate, wn[...], preferred_element_type=F32) + offset[...]
        variance = jnp.mean(pre * pre, axis=1, keepdims=True)
        normed = pre * lax.rsqrt(variance + 1e-05) * scale[...]
        return own.astype(F32) + jnp.maximum(normed, 0.0)

    def paired(micro, source, far_sum, step, at):
        return layer(
            micro,
            source.at[pl.ds(micro * rows, rows)],
            far_sum,
            ws_v.at[step],
            wn_v.at[step],
            bias_v.at[step],
            gain_v.at[step],
            at,
        )

    def zfar(z):
        micro, device = ALONE[z]

        @pl.when(section == device)
        def _():
            far(micro, zagg_v.at[section])

        @pl.when(section != device)
        def _():
            far(micro, zstage_v.at[z])
            zagg_copy(z, section).start()

    def alone():
        for copy in zlocal_in:
            copy.wait()

        @pl.when(twin)
        def _():
            def onward(at, carry):
                depth = 2 * at + side

                @pl.when(depth != section)
                def _():
                    for i in range(len(zparams)):
                        zparam_copy(0, depth, i).wait_recv()
                        zparam_pass(depth, i).start()

                return carry

            lax.fori_loop(0, sections // 2, onward, 0)

        def climb(depth, carry):
            @pl.when(depth != section)
            def _():
                zagg_copy(0, depth).wait_recv()

            @pl.when(
                jnp.logical_and(
                    depth != section, jnp.logical_or(jnp.logical_not(twin), depth % 2 != side)
                )
            )
            def _():
                for i in range(len(zparams)):
                    zparam_copy(0, depth, i).wait_recv()

            for at in range(4):
                value = layer(
                    sole,
                    zx_v.at[depth],
                    zagg_v.at[depth],
                    zws_v.at[depth],
                    zwn_v.at[depth],
                    zbias_v.at[depth],
                    zgain_v.at[depth],
                    at,
                )
                zx_v[depth + 1, at * slab : (at + 1) * slab] = value.astype(BF16)

            @pl.when(jnp.logical_and(depth < last, jnp.logical_and(section > 0, depth + 1 != section)))
            def _():
                zgive(depth + 1).start()

            @pl.when(depth + 1 == section)
            def _():
                zkeep(depth + 1).start()

            return carry

        lax.fori_loop(0, sections, climb, 0)

        @pl.when(section == 0)
        def _():
            pl.semaphore_wait(clear_sem, 1)
            for to in range(1, sections):
                zgive(to).start()

        turn_v[sole] = turned(zx_v[sections])
        for step in ORDER:
            emb_copy(sole, step).start()
        emb_own(sole).start()

    def hop(micro, part):
        at = pl.ds(micro * rows + part * half, half)
        onward = jnp.where(section == 0, 1, jnp.where(section == 1, 2 + micro % 2, section + 2))
        return pltpu.make_async_remote_copy(
            src_ref=out_v.at[at],
            dst_ref=cur_v.at[at],
            send_sem=hop_send.at[micro, part],
            recv_sem=hop_recv.at[micro, part],
            device_id={"section": onward % sections},
            device_id_type=MESH,
        )

    def emb_copy(micro, step):
        to = (section + step) % sections
        return pltpu.make_async_remote_copy(
            src_ref=turn_v.at[micro, pl.ds(to * share, share)],
            dst_ref=emb.at[:, pl.ds(micro * rows, rows)],
            send_sem=emb_send.at[micro, step],
            recv_sem=emb_recv.at[micro],
            device_id={"section": to},
            device_id_type=MESH,
        )

    def turned(block):
        width = block.shape[1]
        row = lax.broadcasted_iota(jnp.int32, (width, width), 0)
        column = lax.broadcasted_iota(jnp.int32, (width, width), 1)
        unit = jnp.where(row == column, 1.0, 0.0).astype(BF16)
        product = lax.dot_general(
            unit, block, (((1,), (1,)), ((), ())), preferred_element_type=F32
        )
        return product.astype(BF16)

    def emb_own(micro):
        return pltpu.make_async_copy(
            turn_v.at[micro, pl.ds(section * share, share)],
            emb.at[:, pl.ds(micro * rows, rows)],
            own_sem.at[micro],
        )

    def keep(micro, source):
        at = pl.ds(micro * rows, rows)
        return pltpu.make_async_copy(source.at[at], fresh.at[at], keep_sem.at[micro])

    def give(micro, source):
        at = pl.ds(micro * rows, rows)
        return pltpu.make_async_remote_copy(
            src_ref=source.at[at],
            dst_ref=fresh.at[at],
            send_sem=give_send.at[micro],
            recv_sem=give_recv.at[micro],
            device_id={"section": sibling},
            device_id_type=MESH,
        )

    def agg_copy(j):
        return pltpu.make_async_remote_copy(
            src_ref=stage_v.at[j],
            dst_ref=agg_v.at[side, j],
            send_sem=agg_send.at[j],
            recv_sem=agg_recv.at[j],
            device_id={"section": sibling},
            device_id_type=MESH,
        )

    @pl.when(first)
    def _():
        @pl.when(section == 0)
        def _():
            feat_in.wait()

        far(0, agg_v.at[0, 0])

        def advance(micro, carry):
            @pl.when(section > 0)
            def _():
                hop(micro, 0).wait_recv()
                hop(micro, 1).wait_recv()

            keep(micro, cur_v).start()
            for part in range(2):
                for at in range(part * 2, (part + 1) * 2):
                    value = paired(micro, cur_v, agg_v.at[0, 0], side, at)
                    out_v[pl.ds(micro * rows + at * slab, slab)] = value.astype(BF16)
                hop(micro, part).start()

            @pl.when(micro < relayed - 1)
            def _():
                far(micro + 1, agg_v.at[0, 0])

            for z in range(len(ALONE)):

                @pl.when(micro == z)
                def _():
                    zfar(z)

            return carry

        lax.fori_loop(0, relayed, advance, 0)

        @pl.when(section == 0)
        def _():
            for micro, _ in ALONE:
                keep(micro, cur_v).start()

        @pl.when(section == 1)
        def _():
            def sent(micro, carry):
                hop(micro, 0).wait_send()
                hop(micro, 1).wait_send()
                return carry

            lax.fori_loop(0, relayed, sent, 0)
            pl.semaphore_signal(clear_sem, inc=1, device_id={"section": sibling}, device_id_type=MESH)

        @pl.when(owner)
        def _():
            alone()

    @pl.when(jnp.logical_not(first))
    def _():
        for z in range(len(ALONE)):
            zfar(z)

        def prepare(j, carry):
            @pl.when(2 * j + 1 - side < relayed)
            def _():
                far(2 * j + 1 - side, stage_v.at[j])
                agg_copy(j).start()

            @pl.when(2 * j + side < relayed)
            def _():
                far(2 * j + side, agg_v.at[side, j])

            return carry

        lax.fori_loop(0, each, prepare, 0)
        for copy in params_out:
            copy.wait_recv()

        @pl.when(owner)
        def _():
            alone()

        def one_pair(j):
            micro = 2 * j + side
            agg_copy(j).wait_recv()
            hop(micro, 0).wait_recv()
            hop(micro, 1).wait_recv()
            for at in range(4):
                value = paired(micro, cur_v, agg_v.at[0, j], 0, at)
                mid_v[pl.ds(micro * rows + at * slab, slab)] = value.astype(BF16)
            for part in range(2):
                for at in range(part * 2, (part + 1) * 2):
                    value = paired(micro, mid_v, agg_v.at[1, j], 1, at)
                    out_v[pl.ds(micro * rows + at * slab, slab)] = value.astype(BF16)

                @pl.when(top)
                def _():
                    at = pl.ds(micro * rows + part * half, half)
                    turn_v[micro, :, part * half : (part + 1) * half] = turned(out_v[at])

                @pl.when(jnp.logical_not(top))
                def _():
                    hop(micro, part).start()

            @pl.when(top)
            def _():
                for step in ORDER:
                    emb_copy(micro, step).start()
                emb_own(micro).start()

            @pl.when(side == 0)
            def _():
                keep(micro, cur_v).start()
                give(micro, mid_v).start()

            @pl.when(side == 1)
            def _():
                keep(micro, mid_v).start()
                give(micro, cur_v).start()

        def advance(j, carry):
            @pl.when(2 * j + side < relayed)
            def _():
                one_pair(j)

            return carry

        lax.fori_loop(0, each, advance, 0)

    for shift in shifts:
        idx_copy(shift, "send").wait_send()
        halo_copy(shift, "send").wait_send()
    @pl.when(first)
    def _():
        def finish(micro, carry):
            keep(micro, cur_v).wait()

            @pl.when(section == 0)
            def _():
                hop(micro, 0).wait_send()
                hop(micro, 1).wait_send()

            return carry

        lax.fori_loop(0, relayed, finish, 0)

        @pl.when(section == 0)
        def _():
            for micro, _ in ALONE:
                keep(micro, cur_v).wait()

    for z, (_, device) in enumerate(ALONE):

        @pl.when(direct(device))
        def _():
            for i in range(len(zparams)):
                zparam_copy(z, section, i).wait_send()

        @pl.when(section != device)
        def _():
            zagg_copy(z, section).wait_send()

            @pl.when(section > 0)
            def _():
                zgot(z).wait_recv()

    @pl.when(owner)
    def _():
        def given(to, carry):
            @pl.when(to != section)
            def _():
                zgive(to).wait_send()

            @pl.when(to == section)
            def _():
                zkeep(to).wait()

            return carry

        lax.fori_loop(1, sections, given, 0)

        @pl.when(twin)
        def _():
            def passed(at, carry):
                depth = 2 * at + side

                @pl.when(depth != section)
                def _():
                    for i in range(len(zparams)):
                        zparam_pass(depth, i).wait_send()

                return carry

            lax.fori_loop(0, sections // 2, passed, 0)

        for step in range(1, sections):
            emb_copy(sole, step).wait_send()
        emb_own(sole).wait()

    @pl.when(jnp.logical_not(first))
    def _():
        for copy in params_out:
            copy.wait_send()

        def finish(j, carry):
            micro = 2 * j + side

            @pl.when(2 * j + 1 - side < relayed)
            def _():
                agg_copy(j).wait_send()
                give(2 * j + 1 - side, cur_v).wait_recv()

            @pl.when(micro < relayed)
            def _():
                keep(micro, cur_v).wait()
                give(micro, cur_v).wait_send()

                @pl.when(jnp.logical_not(top))
                def _():
                    hop(micro, 0).wait_send()
                    hop(micro, 1).wait_send()

                @pl.when(top)
                def _():
                    for step in range(1, sections):
                        emb_copy(micro, step).wait_send()
                    emb_own(micro).wait()

            return carry

        lax.fori_loop(0, each, finish, 0)

    def collect(micro, carry):
        @pl.when(section != sections - 2 + micro % 2)
        def _():
            emb_copy(micro, 1).wait_recv()

        return carry

    lax.fori_loop(0, relayed, collect, 0)
    for micro, device in ALONE:

        @pl.when(section != device)
        def _():
            emb_copy(micro, 1).wait_recv()


def per_device(
    features, history, halo_blocks, tile_values, tile_dst, tile_src, w_self, w_neigh, bias, gain
):
    sections = lax.axis_size("section")
    groups = lax.axis_size("group")
    nodes, width = features.shape
    micros, count, tile = tile_values.shape[:3]
    rows = nodes // micros
    share = width // sections
    dma = pltpu.SemaphoreType.DMA
    hbm = pl.BlockSpec(memory_space=pltpu.HBM)
    vmem = pl.BlockSpec(memory_space=pltpu.VMEM)
    emb, fresh = pl.pallas_call(
        kernel,
        out_shape=(
            pltpu.VMEM((share, nodes), BF16),
            pltpu.VMEM((nodes, width), BF16),
        ),
        in_specs=[hbm] * 10,
        out_specs=(vmem, vmem),
        scratch_shapes=[
            pltpu.SMEM((groups, 1, groups), jnp.int32),
            pltpu.SMEM((1, groups), jnp.int32),
            pltpu.SMEM((micros, 128), jnp.int32),
            pltpu.VMEM((micros, 128), jnp.int32),
            pltpu.VMEM((micros, count), jnp.int32),
            pltpu.VMEM((micros, count), jnp.int32),
            pltpu.VMEM((nodes // tile, tile, width), BF16),
            pltpu.VMEM((micros * count, tile, tile), BF16),
            pltpu.VMEM((groups, tile, width), BF16),
            pltpu.VMEM((groups, tile, width), BF16),
            pltpu.VMEM((micros, rows, rows), BF16),
            pltpu.VMEM((count + 1, tile, tile), F32),
            pltpu.VMEM((count + 1, tile, width), F32),
            pltpu.VMEM((2, micros // 2, rows, width), F32),
            pltpu.VMEM((micros // 2, rows, width), F32),
            pltpu.VMEM((nodes, width), BF16),
            pltpu.VMEM((nodes, width), BF16),
            pltpu.VMEM((nodes, width), BF16),
            pltpu.VMEM((micros, width, rows), BF16),
            pltpu.VMEM((2, width, width), BF16),
            pltpu.VMEM((2, width, width), BF16),
            pltpu.VMEM((2, 1, width), F32),
            pltpu.VMEM((2, 1, width), F32),
            dma((11,)),
            dma((micros,)),
            dma((micros,)),
            dma((groups,)),
            dma((groups,)),
            dma((groups,)),
            dma((groups,)),
            dma((micros, 2)),
            dma((micros, 2)),
            dma((micros, sections)),
            dma((micros,)),
            dma((4,)),
            dma((4,)),
            dma((micros // 2,)),
            dma((micros // 2,)),
            dma((micros,)),
            dma((micros,)),
            pltpu.VMEM((sections + 1, rows, width), BF16),
            pltpu.VMEM((sections, rows, width), BF16),
            pltpu.VMEM((len(ALONE), rows, width), BF16),
            pltpu.VMEM((sections, width, width), BF16),
            pltpu.VMEM((sections, width, width), BF16),
            pltpu.VMEM((sections, 1, width), F32),
            pltpu.VMEM((sections, 1, width), F32),
            dma((6,)),
            dma((len(ALONE), 4)),
            dma((sections, 4)),
            dma((len(ALONE),)),
            dma((sections,)),
            dma((sections,)),
            dma((len(ALONE),)),
            dma((sections, 4)),
            pltpu.SemaphoreType.REGULAR,
        ],
        compiler_params=pltpu.CompilerParams(
            collective_id=0, has_side_effects=True, vmem_limit_bytes=60 * 1024 * 1024
        ),
    )(
        halo_blocks.reshape(1, groups),
        tile_dst,
        tile_src,
        features,
        history.reshape(nodes // tile, tile, width),
        tile_values.reshape(micros * count, tile, tile),
        w_self[0],
        w_neigh[0],
        bias,
        gain,
    )
    return emb.T, fresh.reshape(1, nodes, width)


def solution(mesh):
    placed = (
        P("group", None),
        P("section", "group", None),
        P("group", None, None),
        P("group", None, None, None),
        P("group", None),
        P("group", None),
        P("section", None, None),
        P("section", None, None),
        P("section", None),
        P("section", None),
    )
    return jax.shard_map(
        per_device,
        mesh=mesh,
        in_specs=placed,
        out_specs=(P("group", "section"), P("section", "group", None)),
        check_vma=False,
    )
```

```python
import functools

import jax
import jax.numpy as jnp
from jax import lax
from jax.experimental import pallas as pl
from jax.experimental.pallas import tpu as pltpu
from jax.sharding import PartitionSpec as P

MESH = pl.DeviceIdType.MESH
F32 = jnp.float32
BF16 = jnp.bfloat16
SIDE = 4
ORDER = (4, 5, 3, 6, 2, 7, 1)
ALONE = ((6, 6), (7, 0))


def tile_table(targets, sources, blocks, span):
    micros, count = targets.shape
    key = targets * span + sources
    far_source = jnp.maximum(sources - blocks, 0)
    at = lax.broadcasted_iota(jnp.int32, (micros, count), 1)
    rank = jnp.zeros((micros, count), jnp.int32)
    for j in range(count):
        other = key[:, j : j + 1]
        rank = rank + jnp.where((other < key) | ((other == key) & (at > j)), 1, 0)
    lane = lax.broadcasted_iota(jnp.int32, (micros, 128), 1)
    place = jnp.where(lane < count, lane, lane - count)
    cell = lane - 2 * count
    block = sum(jnp.where(cell >= b * (blocks + 1), 1, 0) for b in range(1, blocks + 1))
    limit = block * span + cell - block * (blocks + 1)
    table = jnp.zeros((micros, 128), jnp.int32)
    for t in range(count):
        chosen = jnp.where(lane < count, t, far_source[:, t : t + 1])
        sorted_part = jnp.where(rank[:, t : t + 1] == place, chosen, 0)
        start_part = jnp.where(key[:, t : t + 1] < limit, 1, 0)
        table = table + jnp.where(lane < 2 * count, sorted_part, start_part)
    return table


def kernel(
    wanted,
    targets,
    sources,
    features,
    history,
    tiles,
    weight_self,
    weight_neigh,
    bias,
    gain,
    emb,
    fresh,
    idx,
    own_idx,
    table,
    table_v,
    dst_v,
    src_v,
    hist_v,
    tiles_v,
    halo_v,
    pack_v,
    dense_v,
    run_tile,
    run_prod,
    agg_v,
    stage_v,
    cur_v,
    mid_v,
    out_v,
    turn_v,
    ws_v,
    wn_v,
    bias_v,
    gain_v,
    local_sem,
    keep_sem,
    own_sem,
    idx_send,
    idx_recv,
    halo_send,
    halo_recv,
    hop_send,
    hop_recv,
    emb_send,
    emb_recv,
    pair_send,
    pair_recv,
    agg_send,
    agg_recv,
    give_send,
    give_recv,
    zx_v,
    zagg_v,
    zstage_v,
    zws_v,
    zwn_v,
    zbias_v,
    zgain_v,
    zlocal,
    zw_send,
    zw_recv,
    zagg_send,
    zagg_recv,
    zgive_send,
    zgive_recv,
    zpass_send,
    clear_sem,
):
    section = lax.axis_index("section")
    group = lax.axis_index("group")
    sections = lax.axis_size("section")
    groups = lax.axis_size("group")
    last = sections - 1
    side = section % 2
    sibling = section + 1 - 2 * side
    first = section < 2
    top = section >= sections - 2
    micros = dense_v.shape[0]
    relayed = micros - len(ALONE)
    each = (relayed + 1) // 2
    devices = [device for _, device in ALONE]
    twins = [device for device in devices if device ^ 1 in devices]
    twin = functools.reduce(jnp.logical_or, [section == device for device in twins], section < 0)
    owner = functools.reduce(jnp.logical_or, [section == device for _, device in ALONE])
    mine = sum(jnp.where(section == device, z, 0) for z, (_, device) in enumerate(ALONE))
    sole = sum(jnp.where(section == device, micro, 0) for micro, device in ALONE)
    count = tiles_v.shape[0] // micros
    rows = dense_v.shape[1]
    half = rows // 2
    slab = half // 2
    tile = tiles_v.shape[1]
    blocks = rows // tile
    share = emb.shape[0]
    gx, gy = group // SIDE, group % SIDE
    shifts = [(dx, dy) for dx in range(SIDE) for dy in range(SIDE) if dx or dy]

    def peer(shift):
        return ((gx + shift[0]) % SIDE) * SIDE + (gy + shift[1]) % SIDE

    def slot(shift):
        return shift[0] * SIDE + shift[1]

    def back(shift):
        return ((-shift[0]) % SIDE, (-shift[1]) % SIDE)

    wanted_in = pltpu.make_async_copy(wanted, own_idx, local_sem.at[0])
    dst_in = pltpu.make_async_copy(targets, dst_v, local_sem.at[1])
    src_in = pltpu.make_async_copy(sources, src_v, local_sem.at[2])
    hist_in = pltpu.make_async_copy(history, hist_v, local_sem.at[3])
    feat_in = pltpu.make_async_copy(features, cur_v, local_sem.at[4])
    tiles_in = pltpu.make_async_copy(tiles, tiles_v, local_sem.at[5])
    params = [(weight_self, ws_v), (weight_neigh, wn_v), (bias, bias_v), (gain, gain_v)]
    params_in = [
        pltpu.make_async_copy(source, target.at[side], local_sem.at[6 + i])
        for i, (source, target) in enumerate(params)
    ]
    for copy in [wanted_in, dst_in, src_in, hist_in] + params_in:
        copy.start()

    @pl.when(section == 0)
    def _():
        feat_in.start()

    tiles_in.start()
    zparams = [(ws_v, zws_v), (wn_v, zwn_v), (bias_v, zbias_v), (gain_v, zgain_v)]
    zlocal_in = [
        pltpu.make_async_copy(features.at[pl.ds(sole * rows, rows)], zx_v.at[0], zlocal.at[4])
    ]

    @pl.when(owner)
    def _():
        for copy in zlocal_in:
            copy.start()

    barrier = pltpu.get_barrier_semaphore()
    for shift in shifts:
        pl.semaphore_signal(barrier, inc=1, device_id={"group": peer(shift)}, device_id_type=MESH)
    for step in range(1, sections):
        pl.semaphore_signal(
            barrier, inc=1, device_id={"section": (section + step) % sections}, device_id_type=MESH
        )

    for copy in params_in:
        copy.wait()
    for target in (ws_v, wn_v, bias_v):
        raw = target[side].astype(F32)
        target[side] = (raw - jnp.mean(raw, axis=1, keepdims=True)).astype(target.dtype)

    @pl.when(owner)
    def _():
        for source, target in zparams:
            target[section] = source[side]

    dst_in.wait()
    src_in.wait()
    table_v[...] = tile_table(dst_v[...], src_v[...], blocks, blocks + groups)
    table_in = pltpu.make_async_copy(table_v, table, local_sem.at[10])
    table_in.start()
    wanted_in.wait()
    pl.semaphore_wait(barrier, groups + sections - 2)

    def idx_copy(shift, way):
        return pltpu.make_async_remote_copy(
            src_ref=own_idx,
            dst_ref=idx.at[group if way == "send" else peer(shift)],
            send_sem=idx_send.at[slot(shift)],
            recv_sem=idx_recv.at[slot(shift if way == "send" else back(shift))],
            device_id={"group": peer(shift)},
            device_id_type=MESH,
        )

    def halo_copy(shift, way):
        return pltpu.make_async_remote_copy(
            src_ref=pack_v.at[slot(shift)],
            dst_ref=halo_v.at[group if way == "send" else peer(shift)],
            send_sem=halo_send.at[slot(shift)],
            recv_sem=halo_recv.at[slot(shift if way == "send" else back(shift))],
            device_id={"group": peer(shift)},
            device_id_type=MESH,
        )

    params_out = [
        pltpu.make_async_remote_copy(
            src_ref=target.at[side],
            dst_ref=target.at[side],
            send_sem=pair_send.at[i],
            recv_sem=pair_recv.at[i],
            device_id={"section": sibling},
            device_id_type=MESH,
        )
        for i, (source, target) in enumerate(params)
    ]

    def zparam_copy(z, at, i):
        source, target = zparams[i]
        return pltpu.make_async_remote_copy(
            src_ref=source.at[side],
            dst_ref=target.at[at],
            send_sem=zw_send.at[z, i],
            recv_sem=zw_recv.at[at, i],
            device_id={"section": ALONE[z][1]},
            device_id_type=MESH,
        )

    def zparam_pass(at, i):
        target = zparams[i][1]
        return pltpu.make_async_remote_copy(
            src_ref=target.at[at],
            dst_ref=target.at[at],
            send_sem=zpass_send.at[at, i],
            recv_sem=zw_recv.at[at, i],
            device_id={"section": sibling},
            device_id_type=MESH,
        )

    def direct(device):
        if device not in twins:
            return section != device
        return jnp.logical_and(
            section != device, jnp.logical_or(side == device % 2, section == device ^ 1)
        )

    def zagg_copy(z, at):
        return pltpu.make_async_remote_copy(
            src_ref=zstage_v.at[z],
            dst_ref=zagg_v.at[at],
            send_sem=zagg_send.at[z],
            recv_sem=zagg_recv.at[at],
            device_id={"section": ALONE[z][1]},
            device_id_type=MESH,
        )

    def zgive(to):
        return pltpu.make_async_remote_copy(
            src_ref=zx_v.at[to],
            dst_ref=fresh.at[pl.ds(sole * rows, rows)],
            send_sem=zgive_send.at[to],
            recv_sem=zgive_recv.at[mine],
            device_id={"section": to},
            device_id_type=MESH,
        )

    def zgot(z):
        at = pl.ds(ALONE[z][0] * rows, rows)
        return pltpu.make_async_remote_copy(
            src_ref=fresh.at[at],
            dst_ref=fresh.at[at],
            send_sem=zgive_send.at[0],
            recv_sem=zgive_recv.at[z],
            device_id={"section": ALONE[z][1]},
            device_id_type=MESH,
        )

    def zkeep(to):
        return pltpu.make_async_copy(
            zx_v.at[to], fresh.at[pl.ds(sole * rows, rows)], zlocal.at[5]
        )

    for shift in shifts:
        idx_copy(shift, "send").start()
    hist_in.wait()
    halo_v[group] = hist_v[own_idx[0, group]]
    for shift in shifts:
        idx_copy(shift, "recv").wait_recv()
        pack_v[slot(shift)] = hist_v[idx[peer(shift), 0, group]]
        halo_copy(shift, "send").start()

    @pl.when(jnp.logical_not(first))
    def _():
        for copy in params_out:
            copy.start()

    for z, (_, device) in enumerate(ALONE):

        @pl.when(direct(device))
        def _():
            for i in range(len(zparams)):
                zparam_copy(z, section, i).start()

    tiles_in.wait()
    table_in.wait()

    zero_tile = jnp.zeros((tile, tile), F32)
    zero_prod = jnp.zeros((tile, ws_v.shape[1]), F32)
    run_tile[0] = zero_tile
    run_prod[0] = zero_prod

    def build(micro, carry):
        total = zero_tile
        for t in range(count):
            total = total + tiles_v[micro * count + table[micro, t]].astype(F32)
            run_tile[t + 1] = total
        for b in range(blocks):
            for s in range(blocks):
                at = 2 * count + b * (blocks + 1) + s
                cell = run_tile[table[micro, at + 1]] - run_tile[table[micro, at]]
                dense_v[micro, b * tile : (b + 1) * tile, s * tile : (s + 1) * tile] = cell.astype(BF16)
        return carry

    lax.fori_loop(0, micros, build, 0)

    for shift in shifts:
        halo_copy(shift, "recv").wait_recv()

    def far(micro, result):
        total = zero_prod
        for t in range(count):
            total = total + jnp.dot(
                tiles_v[micro * count + table[micro, t]],
                halo_v[table[micro, count + t]],
                preferred_element_type=F32,
            )
            run_prod[t + 1] = total
        for b in range(blocks):
            at = 2 * count + b * (blocks + 1) + blocks
            total = run_prod[table[micro, at + 1]] - run_prod[table[micro, at]]
            result[b * tile : (b + 1) * tile] = total.astype(result.dtype)

    def layer(micro, source, far_sum, ws, wn, offset, scale, at):
        own = source[at * slab : (at + 1) * slab]
        near = jnp.dot(
            dense_v[micro, at * slab : (at + 1) * slab], source[...], preferred_element_type=F32
        )
        aggregate = (far_sum[at * slab : (at + 1) * slab].astype(F32) + near).astype(BF16)
        pre = jnp.dot(own, ws[...], preferred_element_type=F32)
        pre = pre + jnp.dot(aggregate, wn[...], preferred_element_type=F32) + offset[...]
        variance = jnp.mean(pre * pre, axis=1, keepdims=True)
        normed = pre * lax.rsqrt(variance + 1e-05) * scale[...]
        return own.astype(F32) + jnp.maximum(normed, 0.0)

    def paired(micro, source, far_sum, step, at):
        return layer(
            micro,
            source.at[pl.ds(micro * rows, rows)],
            far_sum,
            ws_v.at[step],
            wn_v.at[step],
            bias_v.at[step],
            gain_v.at[step],
            at,
        )

    def zfar(z):
        micro, device = ALONE[z]

        @pl.when(section == device)
        def _():
            far(micro, zagg_v.at[section])

        @pl.when(section != device)
        def _():
            far(micro, zstage_v.at[z])
            zagg_copy(z, section).start()

    def alone():
        for copy in zlocal_in:
            copy.wait()

        @pl.when(twin)
        def _():
            def onward(at, carry):
                depth = 2 * at + side

                @pl.when(depth != section)
                def _():
                    for i in range(len(zparams)):
                        zparam_copy(0, depth, i).wait_recv()
                        zparam_pass(depth, i).start()

                return carry

            lax.fori_loop(0, sections // 2, onward, 0)

        def climb(depth, carry):
            @pl.when(depth != section)
            def _():
                zagg_copy(0, depth).wait_recv()

            @pl.when(
                jnp.logical_and(
                    depth != section, jnp.logical_or(jnp.logical_not(twin), depth % 2 != side)
                )
            )
            def _():
                for i in range(len(zparams)):
                    zparam_copy(0, depth, i).wait_recv()

            for at in range(4):
                value = layer(
                    sole,
                    zx_v.at[depth],
                    zagg_v.at[depth],
                    zws_v.at[depth],
                    zwn_v.at[depth],
                    zbias_v.at[depth],
                    zgain_v.at[depth],
                    at,
                )
                zx_v[depth + 1, at * slab : (at + 1) * slab] = value.astype(BF16)

            @pl.when(jnp.logical_and(depth < last, jnp.logical_and(section > 0, depth + 1 != section)))
            def _():
                zgive(depth + 1).start()

            @pl.when(depth + 1 == section)
            def _():
                zkeep(depth + 1).start()

            return carry

        lax.fori_loop(0, sections, climb, 0)

        @pl.when(section == 0)
        def _():
            pl.semaphore_wait(clear_sem, 1)
            for to in range(1, sections):
                zgive(to).start()

        turn_v[sole] = turned(zx_v[sections])
        for step in ORDER:
            emb_copy(sole, step).start()
        emb_own(sole).start()

    def hop(micro):
        at = pl.ds(micro * rows, rows)
        onward = jnp.where(section == 0, 1, jnp.where(section == 1, 2 + micro % 2, section + 2))
        return pltpu.make_async_remote_copy(
            src_ref=out_v.at[at],
            dst_ref=cur_v.at[at],
            send_sem=hop_send.at[micro],
            recv_sem=hop_recv.at[micro],
            device_id={"section": onward % sections},
            device_id_type=MESH,
        )

    def emb_copy(micro, step):
        to = (section + step) % sections
        return pltpu.make_async_remote_copy(
            src_ref=turn_v.at[micro, pl.ds(to * share, share)],
            dst_ref=emb.at[:, pl.ds(micro * rows, rows)],
            send_sem=emb_send.at[micro, step],
            recv_sem=emb_recv.at[micro],
            device_id={"section": to},
            device_id_type=MESH,
        )

    def turned(block):
        width = block.shape[1]
        row = lax.broadcasted_iota(jnp.int32, (width, width), 0)
        column = lax.broadcasted_iota(jnp.int32, (width, width), 1)
        unit = jnp.where(row == column, 1.0, 0.0).astype(BF16)
        product = lax.dot_general(
            unit, block, (((1,), (1,)), ((), ())), preferred_element_type=F32
        )
        return product.astype(BF16)

    def emb_own(micro):
        return pltpu.make_async_copy(
            turn_v.at[micro, pl.ds(section * share, share)],
            emb.at[:, pl.ds(micro * rows, rows)],
            own_sem.at[micro],
        )

    def keep(micro, source):
        at = pl.ds(micro * rows, rows)
        return pltpu.make_async_copy(source.at[at], fresh.at[at], keep_sem.at[micro])

    def give(micro, source):
        at = pl.ds(micro * rows, rows)
        return pltpu.make_async_remote_copy(
            src_ref=source.at[at],
            dst_ref=fresh.at[at],
            send_sem=give_send.at[micro],
            recv_sem=give_recv.at[micro],
            device_id={"section": sibling},
            device_id_type=MESH,
        )

    def agg_copy(j):
        return pltpu.make_async_remote_copy(
            src_ref=stage_v.at[j],
            dst_ref=agg_v.at[side, j],
            send_sem=agg_send.at[j],
            recv_sem=agg_recv.at[j],
            device_id={"section": sibling},
            device_id_type=MESH,
        )

    @pl.when(first)
    def _():
        @pl.when(section == 0)
        def _():
            feat_in.wait()

        far(0, agg_v.at[0, 0])

        def advance(micro, carry):
            @pl.when(section > 0)
            def _():
                hop(micro).wait_recv()

            keep(micro, cur_v).start()
            for at in range(4):
                value = paired(micro, cur_v, agg_v.at[0, 0], side, at)
                out_v[pl.ds(micro * rows + at * slab, slab)] = value.astype(BF16)
            hop(micro).start()

            @pl.when(micro < relayed - 1)
            def _():
                far(micro + 1, agg_v.at[0, 0])

            for z in range(len(ALONE)):

                @pl.when(micro == z)
                def _():
                    zfar(z)

            return carry

        lax.fori_loop(0, relayed, advance, 0)

        @pl.when(section == 0)
        def _():
            for micro, _ in ALONE:
                keep(micro, cur_v).start()

        @pl.when(section == 1)
        def _():
            def sent(micro, carry):
                hop(micro).wait_send()
                return carry

            lax.fori_loop(0, relayed, sent, 0)
            pl.semaphore_signal(clear_sem, inc=1, device_id={"section": sibling}, device_id_type=MESH)

        @pl.when(owner)
        def _():
            alone()

    @pl.when(jnp.logical_not(first))
    def _():
        for z in range(len(ALONE)):
            zfar(z)

        def prepare(j, carry):
            @pl.when(2 * j + 1 - side < relayed)
            def _():
                far(2 * j + 1 - side, stage_v.at[j])
                agg_copy(j).start()

            @pl.when(2 * j + side < relayed)
            def _():
                far(2 * j + side, agg_v.at[side, j])

            return carry

        lax.fori_loop(0, each, prepare, 0)
        for copy in params_out:
            copy.wait_recv()

        @pl.when(owner)
        def _():
            alone()

        def one_pair(j):
            micro = 2 * j + side
            agg_copy(j).wait_recv()
            hop(micro).wait_recv()
            for at in range(4):
                value = paired(micro, cur_v, agg_v.at[0, j], 0, at)
                mid_v[pl.ds(micro * rows + at * slab, slab)] = value.astype(BF16)
            for at in range(4):
                value = paired(micro, mid_v, agg_v.at[1, j], 1, at)
                out_v[pl.ds(micro * rows + at * slab, slab)] = value.astype(BF16)

            @pl.when(jnp.logical_not(top))
            def _():
                hop(micro).start()

            @pl.when(top)
            def _():
                turn_v[micro] = turned(out_v[pl.ds(micro * rows, rows)])
                for step in ORDER:
                    emb_copy(micro, step).start()
                emb_own(micro).start()

            @pl.when(side == 0)
            def _():
                keep(micro, cur_v).start()
                give(micro, mid_v).start()

            @pl.when(side == 1)
            def _():
                keep(micro, mid_v).start()
                give(micro, cur_v).start()

        def advance(j, carry):
            @pl.when(2 * j + side < relayed)
            def _():
                one_pair(j)

            return carry

        lax.fori_loop(0, each, advance, 0)

    for shift in shifts:
        idx_copy(shift, "send").wait_send()
        halo_copy(shift, "send").wait_send()
    @pl.when(first)
    def _():
        def finish(micro, carry):
            keep(micro, cur_v).wait()

            @pl.when(section == 0)
            def _():
                hop(micro).wait_send()

            return carry

        lax.fori_loop(0, relayed, finish, 0)

        @pl.when(section == 0)
        def _():
            for micro, _ in ALONE:
                keep(micro, cur_v).wait()

    for z, (_, device) in enumerate(ALONE):

        @pl.when(direct(device))
        def _():
            for i in range(len(zparams)):
                zparam_copy(z, section, i).wait_send()

        @pl.when(section != device)
        def _():
            zagg_copy(z, section).wait_send()

            @pl.when(section > 0)
            def _():
                zgot(z).wait_recv()

    @pl.when(owner)
    def _():
        def given(to, carry):
            @pl.when(to != section)
            def _():
                zgive(to).wait_send()

            @pl.when(to == section)
            def _():
                zkeep(to).wait()

            return carry

        lax.fori_loop(1, sections, given, 0)

        @pl.when(twin)
        def _():
            def passed(at, carry):
                depth = 2 * at + side

                @pl.when(depth != section)
                def _():
                    for i in range(len(zparams)):
                        zparam_pass(depth, i).wait_send()

                return carry

            lax.fori_loop(0, sections // 2, passed, 0)

        for step in range(1, sections):
            emb_copy(sole, step).wait_send()
        emb_own(sole).wait()

    @pl.when(jnp.logical_not(first))
    def _():
        for copy in params_out:
            copy.wait_send()

        def finish(j, carry):
            micro = 2 * j + side

            @pl.when(2 * j + 1 - side < relayed)
            def _():
                agg_copy(j).wait_send()
                give(2 * j + 1 - side, cur_v).wait_recv()

            @pl.when(micro < relayed)
            def _():
                keep(micro, cur_v).wait()
                give(micro, cur_v).wait_send()

                @pl.when(jnp.logical_not(top))
                def _():
                    hop(micro).wait_send()

                @pl.when(top)
                def _():
                    for step in range(1, sections):
                        emb_copy(micro, step).wait_send()
                    emb_own(micro).wait()

            return carry

        lax.fori_loop(0, each, finish, 0)

    def collect(micro, carry):
        @pl.when(section != sections - 2 + micro % 2)
        def _():
            emb_copy(micro, 1).wait_recv()

        return carry

    lax.fori_loop(0, relayed, collect, 0)
    for micro, device in ALONE:

        @pl.when(section != device)
        def _():
            emb_copy(micro, 1).wait_recv()


def per_device(
    features, history, halo_blocks, tile_values, tile_dst, tile_src, w_self, w_neigh, bias, gain
):
    sections = lax.axis_size("section")
    groups = lax.axis_size("group")
    nodes, width = features.shape
    micros, count, tile = tile_values.shape[:3]
    rows = nodes // micros
    share = width // sections
    dma = pltpu.SemaphoreType.DMA
    hbm = pl.BlockSpec(memory_space=pltpu.HBM)
    vmem = pl.BlockSpec(memory_space=pltpu.VMEM)
    emb, fresh = pl.pallas_call(
        kernel,
        out_shape=(
            pltpu.VMEM((share, nodes), BF16),
            pltpu.VMEM((nodes, width), BF16),
        ),
        in_specs=[hbm] * 10,
        out_specs=(vmem, vmem),
        scratch_shapes=[
            pltpu.SMEM((groups, 1, groups), jnp.int32),
            pltpu.SMEM((1, groups), jnp.int32),
            pltpu.SMEM((micros, 128), jnp.int32),
            pltpu.VMEM((micros, 128), jnp.int32),
            pltpu.VMEM((micros, count), jnp.int32),
            pltpu.VMEM((micros, count), jnp.int32),
            pltpu.VMEM((nodes // tile, tile, width), BF16),
            pltpu.VMEM((micros * count, tile, tile), BF16),
            pltpu.VMEM((groups, tile, width), BF16),
            pltpu.VMEM((groups, tile, width), BF16),
            pltpu.VMEM((micros, rows, rows), BF16),
            pltpu.VMEM((count + 1, tile, tile), F32),
            pltpu.VMEM((count + 1, tile, width), F32),
            pltpu.VMEM((2, micros // 2, rows, width), F32),
            pltpu.VMEM((micros // 2, rows, width), F32),
            pltpu.VMEM((nodes, width), BF16),
            pltpu.VMEM((nodes, width), BF16),
            pltpu.VMEM((nodes, width), BF16),
            pltpu.VMEM((micros, width, rows), BF16),
            pltpu.VMEM((2, width, width), BF16),
            pltpu.VMEM((2, width, width), BF16),
            pltpu.VMEM((2, 1, width), F32),
            pltpu.VMEM((2, 1, width), F32),
            dma((11,)),
            dma((micros,)),
            dma((micros,)),
            dma((groups,)),
            dma((groups,)),
            dma((groups,)),
            dma((groups,)),
            dma((micros,)),
            dma((micros,)),
            dma((micros, sections)),
            dma((micros,)),
            dma((4,)),
            dma((4,)),
            dma((micros // 2,)),
            dma((micros // 2,)),
            dma((micros,)),
            dma((micros,)),
            pltpu.VMEM((sections + 1, rows, width), BF16),
            pltpu.VMEM((sections, rows, width), BF16),
            pltpu.VMEM((len(ALONE), rows, width), BF16),
            pltpu.VMEM((sections, width, width), BF16),
            pltpu.VMEM((sections, width, width), BF16),
            pltpu.VMEM((sections, 1, width), F32),
            pltpu.VMEM((sections, 1, width), F32),
            dma((6,)),
            dma((len(ALONE), 4)),
            dma((sections, 4)),
            dma((len(ALONE),)),
            dma((sections,)),
            dma((sections,)),
            dma((len(ALONE),)),
            dma((sections, 4)),
            pltpu.SemaphoreType.REGULAR,
        ],
        compiler_params=pltpu.CompilerParams(
            collective_id=0, has_side_effects=True, vmem_limit_bytes=60 * 1024 * 1024
        ),
    )(
        halo_blocks.reshape(1, groups),
        tile_dst,
        tile_src,
        features,
        history.reshape(nodes // tile, tile, width),
        tile_values.reshape(micros * count, tile, tile),
        w_self[0],
        w_neigh[0],
        bias,
        gain,
    )
    return emb.T, fresh.reshape(1, nodes, width)


def solution(mesh):
    placed = (
        P("group", None),
        P("section", "group", None),
        P("group", None, None),
        P("group", None, None, None),
        P("group", None),
        P("group", None),
        P("section", None, None),
        P("section", None, None),
        P("section", None),
        P("section", None),
    )
    return jax.shard_map(
        per_device,
        mesh=mesh,
        in_specs=placed,
        out_specs=(P("group", "section"), P("section", "group", None)),
        check_vma=False,
    )
```

```python
import functools

import jax
import jax.numpy as jnp
from jax import lax
from jax.experimental import pallas as pl
from jax.experimental.pallas import tpu as pltpu
from jax.sharding import PartitionSpec as P

MESH = pl.DeviceIdType.MESH
F32 = jnp.float32
BF16 = jnp.bfloat16
SIDE = 4
ORDER = (4, 5, 3, 6, 2, 7, 1)
ALONE = ((6, 6), (7, 0))


def tile_table(targets, sources, blocks, span):
    micros, count = targets.shape
    key = targets * span + sources
    far_source = jnp.maximum(sources - blocks, 0)
    at = lax.broadcasted_iota(jnp.int32, (micros, count), 1)
    rank = jnp.zeros((micros, count), jnp.int32)
    for j in range(count):
        other = key[:, j : j + 1]
        rank = rank + jnp.where((other < key) | ((other == key) & (at > j)), 1, 0)
    lane = lax.broadcasted_iota(jnp.int32, (micros, 128), 1)
    place = jnp.where(lane < count, lane, lane - count)
    cell = lane - 2 * count
    block = sum(jnp.where(cell >= b * (blocks + 1), 1, 0) for b in range(1, blocks + 1))
    limit = block * span + cell - block * (blocks + 1)
    table = jnp.zeros((micros, 128), jnp.int32)
    for t in range(count):
        chosen = jnp.where(lane < count, t, far_source[:, t : t + 1])
        sorted_part = jnp.where(rank[:, t : t + 1] == place, chosen, 0)
        start_part = jnp.where(key[:, t : t + 1] < limit, 1, 0)
        table = table + jnp.where(lane < 2 * count, sorted_part, start_part)
    return table


def kernel(
    wanted,
    targets,
    sources,
    features,
    history,
    tiles,
    weight_self,
    weight_neigh,
    bias,
    gain,
    emb,
    fresh,
    idx,
    own_idx,
    table,
    table_v,
    dst_v,
    src_v,
    hist_v,
    tiles_v,
    halo_v,
    pack_v,
    dense_v,
    run_tile,
    run_prod,
    agg_v,
    stage_v,
    cur_v,
    mid_v,
    out_v,
    turn_v,
    ws_v,
    wn_v,
    bias_v,
    gain_v,
    local_sem,
    keep_sem,
    own_sem,
    idx_send,
    idx_recv,
    halo_send,
    halo_recv,
    hop_send,
    hop_recv,
    emb_send,
    emb_recv,
    pair_send,
    pair_recv,
    agg_send,
    agg_recv,
    give_send,
    give_recv,
    zx_v,
    zagg_v,
    zstage_v,
    zws_v,
    zwn_v,
    zbias_v,
    zgain_v,
    zlocal,
    zw_send,
    zw_recv,
    zagg_send,
    zagg_recv,
    zgive_send,
    zgive_recv,
    zpass_send,
    clear_sem,
):
    section = lax.axis_index("section")
    group = lax.axis_index("group")
    sections = lax.axis_size("section")
    groups = lax.axis_size("group")
    last = sections - 1
    side = section % 2
    sibling = section + 1 - 2 * side
    first = section < 2
    top = section >= sections - 2
    micros = dense_v.shape[0]
    relayed = micros - len(ALONE)
    each = (relayed + 1) // 2
    devices = [device for _, device in ALONE]
    twins = [device for device in devices if device ^ 1 in devices]
    twin = functools.reduce(jnp.logical_or, [section == device for device in twins], section < 0)
    owner = functools.reduce(jnp.logical_or, [section == device for _, device in ALONE])
    mine = sum(jnp.where(section == device, z, 0) for z, (_, device) in enumerate(ALONE))
    sole = sum(jnp.where(section == device, micro, 0) for micro, device in ALONE)
    count = tiles_v.shape[0] // micros
    rows = dense_v.shape[1]
    half = rows // 2
    slab = half // 2
    tile = tiles_v.shape[1]
    blocks = rows // tile
    share = emb.shape[0]
    gx, gy = group // SIDE, group % SIDE
    shifts = [(dx, dy) for dx in range(SIDE) for dy in range(SIDE) if dx or dy]

    def peer(shift):
        return ((gx + shift[0]) % SIDE) * SIDE + (gy + shift[1]) % SIDE

    def slot(shift):
        return shift[0] * SIDE + shift[1]

    def back(shift):
        return ((-shift[0]) % SIDE, (-shift[1]) % SIDE)

    wanted_in = pltpu.make_async_copy(wanted, own_idx, local_sem.at[0])
    dst_in = pltpu.make_async_copy(targets, dst_v, local_sem.at[1])
    src_in = pltpu.make_async_copy(sources, src_v, local_sem.at[2])
    hist_in = pltpu.make_async_copy(history, hist_v, local_sem.at[3])
    feat_in = pltpu.make_async_copy(features, cur_v, local_sem.at[4])
    tiles_in = pltpu.make_async_copy(tiles, tiles_v, local_sem.at[5])
    params = [(weight_self, ws_v), (weight_neigh, wn_v), (bias, bias_v), (gain, gain_v)]
    params_in = [
        pltpu.make_async_copy(source, target.at[side], local_sem.at[6 + i])
        for i, (source, target) in enumerate(params)
    ]
    for copy in [wanted_in, dst_in, src_in, hist_in] + params_in:
        copy.start()

    @pl.when(section == 0)
    def _():
        feat_in.start()

    tiles_in.start()
    zparams = [(ws_v, zws_v), (wn_v, zwn_v), (bias_v, zbias_v), (gain_v, zgain_v)]
    zlocal_in = [
        pltpu.make_async_copy(features.at[pl.ds(sole * rows, rows)], zx_v.at[0], zlocal.at[4])
    ]

    @pl.when(owner)
    def _():
        for copy in zlocal_in:
            copy.start()

    barrier = pltpu.get_barrier_semaphore()
    for shift in shifts:
        pl.semaphore_signal(barrier, inc=1, device_id={"group": peer(shift)}, device_id_type=MESH)
    for step in range(1, sections):
        pl.semaphore_signal(
            barrier, inc=1, device_id={"section": (section + step) % sections}, device_id_type=MESH
        )

    for copy in params_in:
        copy.wait()
    for target in (ws_v, wn_v, bias_v):
        raw = target[side].astype(F32)
        target[side] = (raw - jnp.mean(raw, axis=1, keepdims=True)).astype(target.dtype)

    @pl.when(owner)
    def _():
        for source, target in zparams:
            target[section] = source[side]

    dst_in.wait()
    src_in.wait()
    table_v[...] = tile_table(dst_v[...], src_v[...], blocks, blocks + groups)
    table_in = pltpu.make_async_copy(table_v, table, local_sem.at[10])
    table_in.start()
    wanted_in.wait()
    pl.semaphore_wait(barrier, groups + sections - 2)

    def idx_copy(shift, way):
        return pltpu.make_async_remote_copy(
            src_ref=own_idx,
            dst_ref=idx.at[group if way == "send" else peer(shift)],
            send_sem=idx_send.at[slot(shift)],
            recv_sem=idx_recv.at[slot(shift if way == "send" else back(shift))],
            device_id={"group": peer(shift)},
            device_id_type=MESH,
        )

    def halo_copy(shift, way):
        return pltpu.make_async_remote_copy(
            src_ref=pack_v.at[slot(shift)],
            dst_ref=halo_v.at[group if way == "send" else peer(shift)],
            send_sem=halo_send.at[slot(shift)],
            recv_sem=halo_recv.at[slot(shift if way == "send" else back(shift))],
            device_id={"group": peer(shift)},
            device_id_type=MESH,
        )

    params_out = [
        pltpu.make_async_remote_copy(
            src_ref=target.at[side],
            dst_ref=target.at[side],
            send_sem=pair_send.at[i],
            recv_sem=pair_recv.at[i],
            device_id={"section": sibling},
            device_id_type=MESH,
        )
        for i, (source, target) in enumerate(params)
    ]

    def zparam_copy(z, at, i):
        source, target = zparams[i]
        return pltpu.make_async_remote_copy(
            src_ref=source.at[side],
            dst_ref=target.at[at],
            send_sem=zw_send.at[z, i],
            recv_sem=zw_recv.at[at, i],
            device_id={"section": ALONE[z][1]},
            device_id_type=MESH,
        )

    def zparam_pass(at, i):
        target = zparams[i][1]
        return pltpu.make_async_remote_copy(
            src_ref=target.at[at],
            dst_ref=target.at[at],
            send_sem=zpass_send.at[at, i],
            recv_sem=zw_recv.at[at, i],
            device_id={"section": sibling},
            device_id_type=MESH,
        )

    def direct(device):
        if device not in twins:
            return section != device
        return jnp.logical_and(
            section != device, jnp.logical_or(side == device % 2, section == device ^ 1)
        )

    def zagg_copy(z, at):
        return pltpu.make_async_remote_copy(
            src_ref=zstage_v.at[z],
            dst_ref=zagg_v.at[at],
            send_sem=zagg_send.at[z],
            recv_sem=zagg_recv.at[at],
            device_id={"section": ALONE[z][1]},
            device_id_type=MESH,
        )

    def zgive(to):
        return pltpu.make_async_remote_copy(
            src_ref=zx_v.at[to],
            dst_ref=fresh.at[pl.ds(sole * rows, rows)],
            send_sem=zgive_send.at[to],
            recv_sem=zgive_recv.at[mine],
            device_id={"section": to},
            device_id_type=MESH,
        )

    def zgot(z):
        at = pl.ds(ALONE[z][0] * rows, rows)
        return pltpu.make_async_remote_copy(
            src_ref=fresh.at[at],
            dst_ref=fresh.at[at],
            send_sem=zgive_send.at[0],
            recv_sem=zgive_recv.at[z],
            device_id={"section": ALONE[z][1]},
            device_id_type=MESH,
        )

    def zkeep(to):
        return pltpu.make_async_copy(
            zx_v.at[to], fresh.at[pl.ds(sole * rows, rows)], zlocal.at[5]
        )

    for shift in shifts:
        idx_copy(shift, "send").start()
    hist_in.wait()
    halo_v[group] = hist_v[own_idx[0, group]]
    for shift in shifts:
        idx_copy(shift, "recv").wait_recv()
        pack_v[slot(shift)] = hist_v[idx[peer(shift), 0, group]]
        halo_copy(shift, "send").start()

    tiles_in.wait()
    table_in.wait()

    zero_tile = jnp.zeros((tile, tile), F32)
    zero_prod = jnp.zeros((tile, ws_v.shape[1]), F32)
    run_tile[0] = zero_tile
    run_prod[0] = zero_prod

    def build(micro, carry):
        total = zero_tile
        for t in range(count):
            total = total + tiles_v[micro * count + table[micro, t]].astype(F32)
            run_tile[t + 1] = total
        for b in range(blocks):
            for s in range(blocks):
                at = 2 * count + b * (blocks + 1) + s
                cell = run_tile[table[micro, at + 1]] - run_tile[table[micro, at]]
                dense_v[micro, b * tile : (b + 1) * tile, s * tile : (s + 1) * tile] = cell.astype(BF16)
        return carry

    lax.fori_loop(0, micros, build, 0)

    @pl.when(jnp.logical_not(first))
    def _():
        for copy in params_out:
            copy.start()

    for z, (_, device) in enumerate(ALONE):

        @pl.when(direct(device))
        def _():
            for i in range(len(zparams)):
                zparam_copy(z, section, i).start()

    for shift in shifts:
        halo_copy(shift, "recv").wait_recv()

    def far(micro, result):
        total = zero_prod
        for t in range(count):
            total = total + jnp.dot(
                tiles_v[micro * count + table[micro, t]],
                halo_v[table[micro, count + t]],
                preferred_element_type=F32,
            )
            run_prod[t + 1] = total
        for b in range(blocks):
            at = 2 * count + b * (blocks + 1) + blocks
            total = run_prod[table[micro, at + 1]] - run_prod[table[micro, at]]
            result[b * tile : (b + 1) * tile] = total.astype(result.dtype)

    def layer(micro, source, far_sum, ws, wn, offset, scale, at):
        own = source[at * slab : (at + 1) * slab]
        near = jnp.dot(
            dense_v[micro, at * slab : (at + 1) * slab], source[...], preferred_element_type=F32
        )
        aggregate = (far_sum[at * slab : (at + 1) * slab].astype(F32) + near).astype(BF16)
        pre = jnp.dot(own, ws[...], preferred_element_type=F32)
        pre = pre + jnp.dot(aggregate, wn[...], preferred_element_type=F32) + offset[...]
        variance = jnp.mean(pre * pre, axis=1, keepdims=True)
        normed = pre * lax.rsqrt(variance + 1e-05) * scale[...]
        return own.astype(F32) + jnp.maximum(normed, 0.0)

    def paired(micro, source, far_sum, step, at):
        return layer(
            micro,
            source.at[pl.ds(micro * rows, rows)],
            far_sum,
            ws_v.at[step],
            wn_v.at[step],
            bias_v.at[step],
            gain_v.at[step],
            at,
        )

    def zfar(z):
        micro, device = ALONE[z]

        @pl.when(section == device)
        def _():
            far(micro, zagg_v.at[section])

        @pl.when(section != device)
        def _():
            far(micro, zstage_v.at[z])
            zagg_copy(z, section).start()

    def alone():
        for copy in zlocal_in:
            copy.wait()

        @pl.when(twin)
        def _():
            def onward(at, carry):
                depth = 2 * at + side

                @pl.when(depth != section)
                def _():
                    for i in range(len(zparams)):
                        zparam_copy(0, depth, i).wait_recv()
                        zparam_pass(depth, i).start()

                return carry

            lax.fori_loop(0, sections // 2, onward, 0)

        def climb(depth, carry):
            @pl.when(depth != section)
            def _():
                zagg_copy(0, depth).wait_recv()

            @pl.when(
                jnp.logical_and(
                    depth != section, jnp.logical_or(jnp.logical_not(twin), depth % 2 != side)
                )
            )
            def _():
                for i in range(len(zparams)):
                    zparam_copy(0, depth, i).wait_recv()

            for at in range(4):
                value = layer(
                    sole,
                    zx_v.at[depth],
                    zagg_v.at[depth],
                    zws_v.at[depth],
                    zwn_v.at[depth],
                    zbias_v.at[depth],
                    zgain_v.at[depth],
                    at,
                )
                zx_v[depth + 1, at * slab : (at + 1) * slab] = value.astype(BF16)

            @pl.when(jnp.logical_and(depth < last, jnp.logical_and(section > 0, depth + 1 != section)))
            def _():
                zgive(depth + 1).start()

            @pl.when(depth + 1 == section)
            def _():
                zkeep(depth + 1).start()

            return carry

        lax.fori_loop(0, sections, climb, 0)

        @pl.when(section == 0)
        def _():
            pl.semaphore_wait(clear_sem, 1)
            for to in range(1, sections):
                zgive(to).start()

        turn_v[sole] = turned(zx_v[sections])
        for step in ORDER:
            emb_copy(sole, step).start()
        emb_own(sole).start()

    def hop(micro):
        at = pl.ds(micro * rows, rows)
        onward = jnp.where(section == 0, 1, jnp.where(section == 1, 2 + micro % 2, section + 2))
        return pltpu.make_async_remote_copy(
            src_ref=out_v.at[at],
            dst_ref=cur_v.at[at],
            send_sem=hop_send.at[micro],
            recv_sem=hop_recv.at[micro],
            device_id={"section": onward % sections},
            device_id_type=MESH,
        )

    def emb_copy(micro, step):
        to = (section + step) % sections
        return pltpu.make_async_remote_copy(
            src_ref=turn_v.at[micro, pl.ds(to * share, share)],
            dst_ref=emb.at[:, pl.ds(micro * rows, rows)],
            send_sem=emb_send.at[micro, step],
            recv_sem=emb_recv.at[micro],
            device_id={"section": to},
            device_id_type=MESH,
        )

    def turned(block):
        width = block.shape[1]
        row = lax.broadcasted_iota(jnp.int32, (width, width), 0)
        column = lax.broadcasted_iota(jnp.int32, (width, width), 1)
        unit = jnp.where(row == column, 1.0, 0.0).astype(BF16)
        product = lax.dot_general(
            unit, block, (((1,), (1,)), ((), ())), preferred_element_type=F32
        )
        return product.astype(BF16)

    def emb_own(micro):
        return pltpu.make_async_copy(
            turn_v.at[micro, pl.ds(section * share, share)],
            emb.at[:, pl.ds(micro * rows, rows)],
            own_sem.at[micro],
        )

    def keep(micro, source):
        at = pl.ds(micro * rows, rows)
        return pltpu.make_async_copy(source.at[at], fresh.at[at], keep_sem.at[micro])

    def give(micro, source):
        at = pl.ds(micro * rows, rows)
        return pltpu.make_async_remote_copy(
            src_ref=source.at[at],
            dst_ref=fresh.at[at],
            send_sem=give_send.at[micro],
            recv_sem=give_recv.at[micro],
            device_id={"section": sibling},
            device_id_type=MESH,
        )

    def agg_copy(j):
        return pltpu.make_async_remote_copy(
            src_ref=stage_v.at[j],
            dst_ref=agg_v.at[side, j],
            send_sem=agg_send.at[j],
            recv_sem=agg_recv.at[j],
            device_id={"section": sibling},
            device_id_type=MESH,
        )

    @pl.when(first)
    def _():
        @pl.when(section == 0)
        def _():
            feat_in.wait()

        far(0, agg_v.at[0, 0])

        def advance(micro, carry):
            @pl.when(section > 0)
            def _():
                hop(micro).wait_recv()

            keep(micro, cur_v).start()
            for at in range(4):
                value = paired(micro, cur_v, agg_v.at[0, 0], side, at)
                out_v[pl.ds(micro * rows + at * slab, slab)] = value.astype(BF16)
            hop(micro).start()

            @pl.when(micro < relayed - 1)
            def _():
                far(micro + 1, agg_v.at[0, 0])

            for z in range(len(ALONE)):

                @pl.when(micro == z)
                def _():
                    zfar(z)

            return carry

        lax.fori_loop(0, relayed, advance, 0)

        @pl.when(section == 0)
        def _():
            for micro, _ in ALONE:
                keep(micro, cur_v).start()

        @pl.when(section == 1)
        def _():
            def sent(micro, carry):
                hop(micro).wait_send()
                return carry

            lax.fori_loop(0, relayed, sent, 0)
            pl.semaphore_signal(clear_sem, inc=1, device_id={"section": sibling}, device_id_type=MESH)

        @pl.when(owner)
        def _():
            alone()

    @pl.when(jnp.logical_not(first))
    def _():
        for z in range(len(ALONE)):
            zfar(z)

        def prepare(j, carry):
            @pl.when(2 * j + 1 - side < relayed)
            def _():
                far(2 * j + 1 - side, stage_v.at[j])
                agg_copy(j).start()

            @pl.when(2 * j + side < relayed)
            def _():
                far(2 * j + side, agg_v.at[side, j])

            return carry

        lax.fori_loop(0, each, prepare, 0)
        for copy in params_out:
            copy.wait_recv()

        @pl.when(owner)
        def _():
            alone()

        def one_pair(j):
            micro = 2 * j + side
            agg_copy(j).wait_recv()
            hop(micro).wait_recv()
            for at in range(4):
                value = paired(micro, cur_v, agg_v.at[0, j], 0, at)
                mid_v[pl.ds(micro * rows + at * slab, slab)] = value.astype(BF16)
            for at in range(4):
                value = paired(micro, mid_v, agg_v.at[1, j], 1, at)
                out_v[pl.ds(micro * rows + at * slab, slab)] = value.astype(BF16)

            @pl.when(jnp.logical_not(top))
            def _():
                hop(micro).start()

            @pl.when(top)
            def _():
                turn_v[micro] = turned(out_v[pl.ds(micro * rows, rows)])
                for step in ORDER:
                    emb_copy(micro, step).start()
                emb_own(micro).start()

            @pl.when(side == 0)
            def _():
                keep(micro, cur_v).start()
                give(micro, mid_v).start()

            @pl.when(side == 1)
            def _():
                keep(micro, mid_v).start()
                give(micro, cur_v).start()

        def advance(j, carry):
            @pl.when(2 * j + side < relayed)
            def _():
                one_pair(j)

            return carry

        lax.fori_loop(0, each, advance, 0)

    for shift in shifts:
        idx_copy(shift, "send").wait_send()
        halo_copy(shift, "send").wait_send()
    @pl.when(first)
    def _():
        def finish(micro, carry):
            keep(micro, cur_v).wait()

            @pl.when(section == 0)
            def _():
                hop(micro).wait_send()

            return carry

        lax.fori_loop(0, relayed, finish, 0)

        @pl.when(section == 0)
        def _():
            for micro, _ in ALONE:
                keep(micro, cur_v).wait()

    for z, (_, device) in enumerate(ALONE):

        @pl.when(direct(device))
        def _():
            for i in range(len(zparams)):
                zparam_copy(z, section, i).wait_send()

        @pl.when(section != device)
        def _():
            zagg_copy(z, section).wait_send()

            @pl.when(section > 0)
            def _():
                zgot(z).wait_recv()

    @pl.when(owner)
    def _():
        def given(to, carry):
            @pl.when(to != section)
            def _():
                zgive(to).wait_send()

            @pl.when(to == section)
            def _():
                zkeep(to).wait()

            return carry

        lax.fori_loop(1, sections, given, 0)

        @pl.when(twin)
        def _():
            def passed(at, carry):
                depth = 2 * at + side

                @pl.when(depth != section)
                def _():
                    for i in range(len(zparams)):
                        zparam_pass(depth, i).wait_send()

                return carry

            lax.fori_loop(0, sections // 2, passed, 0)

        for step in range(1, sections):
            emb_copy(sole, step).wait_send()
        emb_own(sole).wait()

    @pl.when(jnp.logical_not(first))
    def _():
        for copy in params_out:
            copy.wait_send()

        def finish(j, carry):
            micro = 2 * j + side

            @pl.when(2 * j + 1 - side < relayed)
            def _():
                agg_copy(j).wait_send()
                give(2 * j + 1 - side, cur_v).wait_recv()

            @pl.when(micro < relayed)
            def _():
                keep(micro, cur_v).wait()
                give(micro, cur_v).wait_send()

                @pl.when(jnp.logical_not(top))
                def _():
                    hop(micro).wait_send()

                @pl.when(top)
                def _():
                    for step in range(1, sections):
                        emb_copy(micro, step).wait_send()
                    emb_own(micro).wait()

            return carry

        lax.fori_loop(0, each, finish, 0)

    def collect(micro, carry):
        @pl.when(section != sections - 2 + micro % 2)
        def _():
            emb_copy(micro, 1).wait_recv()

        return carry

    lax.fori_loop(0, relayed, collect, 0)
    for micro, device in ALONE:

        @pl.when(section != device)
        def _():
            emb_copy(micro, 1).wait_recv()


def per_device(
    features, history, halo_blocks, tile_values, tile_dst, tile_src, w_self, w_neigh, bias, gain
):
    sections = lax.axis_size("section")
    groups = lax.axis_size("group")
    nodes, width = features.shape
    micros, count, tile = tile_values.shape[:3]
    rows = nodes // micros
    share = width // sections
    dma = pltpu.SemaphoreType.DMA
    hbm = pl.BlockSpec(memory_space=pltpu.HBM)
    vmem = pl.BlockSpec(memory_space=pltpu.VMEM)
    emb, fresh = pl.pallas_call(
        kernel,
        out_shape=(
            pltpu.VMEM((share, nodes), BF16),
            pltpu.VMEM((nodes, width), BF16),
        ),
        in_specs=[hbm] * 10,
        out_specs=(vmem, vmem),
        scratch_shapes=[
            pltpu.SMEM((groups, 1, groups), jnp.int32),
            pltpu.SMEM((1, groups), jnp.int32),
            pltpu.SMEM((micros, 128), jnp.int32),
            pltpu.VMEM((micros, 128), jnp.int32),
            pltpu.VMEM((micros, count), jnp.int32),
            pltpu.VMEM((micros, count), jnp.int32),
            pltpu.VMEM((nodes // tile, tile, width), BF16),
            pltpu.VMEM((micros * count, tile, tile), BF16),
            pltpu.VMEM((groups, tile, width), BF16),
            pltpu.VMEM((groups, tile, width), BF16),
            pltpu.VMEM((micros, rows, rows), BF16),
            pltpu.VMEM((count + 1, tile, tile), F32),
            pltpu.VMEM((count + 1, tile, width), F32),
            pltpu.VMEM((2, micros // 2, rows, width), F32),
            pltpu.VMEM((micros // 2, rows, width), F32),
            pltpu.VMEM((nodes, width), BF16),
            pltpu.VMEM((nodes, width), BF16),
            pltpu.VMEM((nodes, width), BF16),
            pltpu.VMEM((micros, width, rows), BF16),
            pltpu.VMEM((2, width, width), BF16),
            pltpu.VMEM((2, width, width), BF16),
            pltpu.VMEM((2, 1, width), F32),
            pltpu.VMEM((2, 1, width), F32),
            dma((11,)),
            dma((micros,)),
            dma((micros,)),
            dma((groups,)),
            dma((groups,)),
            dma((groups,)),
            dma((groups,)),
            dma((micros,)),
            dma((micros,)),
            dma((micros, sections)),
            dma((micros,)),
            dma((4,)),
            dma((4,)),
            dma((micros // 2,)),
            dma((micros // 2,)),
            dma((micros,)),
            dma((micros,)),
            pltpu.VMEM((sections + 1, rows, width), BF16),
            pltpu.VMEM((sections, rows, width), BF16),
            pltpu.VMEM((len(ALONE), rows, width), BF16),
            pltpu.VMEM((sections, width, width), BF16),
            pltpu.VMEM((sections, width, width), BF16),
            pltpu.VMEM((sections, 1, width), F32),
            pltpu.VMEM((sections, 1, width), F32),
            dma((6,)),
            dma((len(ALONE), 4)),
            dma((sections, 4)),
            dma((len(ALONE),)),
            dma((sections,)),
            dma((sections,)),
            dma((len(ALONE),)),
            dma((sections, 4)),
            pltpu.SemaphoreType.REGULAR,
        ],
        compiler_params=pltpu.CompilerParams(
            collective_id=0, has_side_effects=True, vmem_limit_bytes=60 * 1024 * 1024
        ),
    )(
        halo_blocks.reshape(1, groups),
        tile_dst,
        tile_src,
        features,
        history.reshape(nodes // tile, tile, width),
        tile_values.reshape(micros * count, tile, tile),
        w_self[0],
        w_neigh[0],
        bias,
        gain,
    )
    return emb.T, fresh.reshape(1, nodes, width)


def solution(mesh):
    placed = (
        P("group", None),
        P("section", "group", None),
        P("group", None, None),
        P("group", None, None, None),
        P("group", None),
        P("group", None),
        P("section", None, None),
        P("section", None, None),
        P("section", None),
        P("section", None),
    )
    return jax.shard_map(
        per_device,
        mesh=mesh,
        in_specs=placed,
        out_specs=(P("group", "section"), P("section", "group", None)),
        check_vma=False,
    )
```
